32 devices in a mesh: pos: 16 (over z, y, x), head: 2 (over core).
Axes of the slice: x: 2, y: 2, z: 4, core: 2. Of those that a mesh axis runs over, the one named last changes fastest.
Arguments:
- token_ids: int32 [16384], P('pos'), may hold values from 0 to 255
- token_table: float32 [256, 1024], replicated, may hold values from -6 to 6
- row_table: float32 [256, 1024], replicated, may hold values from -6 to 6
- col_table: float32 [256, 1024], replicated, may hold values from -6 to 6
- chan_table: float32 [3, 1024], replicated, may hold values from -6 to 6
- w_query: float32 [1024, 1024], P(None, 'head'), as said below
- w_key: float32 [1024, 1024], P(None, 'head'), as said below
- w_value: float32 [1024, 1024], P(None, 'head'), may hold values from -0.1875 to 0.1875
- w_out: float32 [1024, 1024], P('head', 'pos'), may hold values from -0.1875 to 0.1875
- w_in: float32 [1024, 4096], P('pos', 'head'), may hold values from -0.1875 to 0.1875
- w_down: float32 [4096, 1024], P('head', 'pos'), may hold values from -0.09375 to 0.09375
Outputs:
- latent_out: float32 [512, 1024], P('pos')
The draws below stay inside these ranges and needn't reach their ends.
Inputs may be any that keep to these rules, and one draw needn't show every extreme that they name: `w_query`: entries of order 1024^-0.5 times a few. `w_key`: entries of order 1024^-0.5 times a few, or larger.
All inputs are finite; a program needn't handle non-finite values.
Results may differ from the reference program's by a relative error of at most 0.0003.
Values sent between devices are 32-bit elements; how exact they have to be, the bound alone decides.
A program may use at most 128 MiB of HBM per device.

```python
import jax
import jax.numpy as jnp
from jax import lax

D = 1024
HEADS = 16
HD = 64
FF = 4096
VOCAB = 256
IMG = 256
LAT = 512
POS_DEV = 1024
POSITIONS = 16384


def query_key_pair(key):
    first = jnp.clip(jax.random.normal(jax.random.fold_in(key, 11), (D, HEADS * HD), jnp.float32), -6.0, 6.0) * D ** (-0.5)
    second = jnp.clip(jax.random.normal(jax.random.fold_in(key, 12), (D, HEADS * HD), jnp.float32), -6.0, 6.0) * D ** (-0.5)
    return (first, second)


def draw_w_query(key, part):
    first, second = query_key_pair(key)
    return first


def draw_w_key(key, part):
    first, second = query_key_pair(key)
    return second


def place_ends(result, rng, least, largest):
    longest = result.shape.index(max(result.shape))
    spots = []
    for shift in (0, 1):
        where = [jax.random.randint(jax.random.fold_in(rng, axis), (), 0, length) for axis, length in enumerate(result.shape)]
        where[longest] = (where[longest] + shift) % result.shape[longest]
        spots.append(tuple(where))
    return result.at[spots[0]].set(least).at[spots[1]].set(largest)


def levels(own_key, dims, split, smallest, high):
    def one(axis_at, blocks):
        steps = jax.random.uniform(jax.random.fold_in(jax.random.fold_in(own_key, 6), axis_at), (blocks,), jnp.float32, smallest / len(split), high / len(split))
        return jnp.repeat(jnp.exp(steps), dims[axis_at] // blocks).reshape((-1,) + (1,) * (len(dims) - axis_at - 1))

    loudness = one(*split[0])
    for cut in split[1:]:
        loudness = loudness * one(*cut)
    return loudness


def bell_draw(own_key, shape, deviation, most, shards=(), kind=jnp.bfloat16):
    values = deviation * jax.random.normal(own_key, shape, jnp.float32)
    if shards:
        values = values * levels(own_key, shape, shards, -0.22, 0.18)
    return jnp.clip(values, -most, most).astype(kind)


def setup_inputs(seed: int = 0) -> dict:
    splits = jax.random.split(jax.random.key(seed), 12)
    token_ids = place_ends(jax.random.randint(splits[0], (POSITIONS,), 0, VOCAB), jax.random.fold_in(splits[0], 1), 0, VOCAB - 1).astype(jnp.int32)
    token_table = bell_draw(splits[1], (VOCAB, D), 1.0, 6.0, (), jnp.float32)
    row_table = bell_draw(splits[2], (IMG, D), 1.0, 6.0, (), jnp.float32)
    col_table = bell_draw(splits[3], (IMG, D), 1.0, 6.0, (), jnp.float32)
    chan_table = bell_draw(splits[4], (3, D), 1.0, 6.0, (), jnp.float32)
    w_query = draw_w_query(jax.random.fold_in(splits[11], 71), 0)
    w_key = draw_w_key(jax.random.fold_in(splits[11], 71), 0)
    w_value = bell_draw(splits[7], (D, HEADS * HD), D ** -0.5, 0.1875, ((1, 2),), jnp.float32)
    w_out = bell_draw(splits[8], (HEADS * HD, D), (HEADS * HD) ** -0.5, 0.1875, ((0, 2), (1, 16)), jnp.float32)
    w_in = bell_draw(splits[9], (D, FF), D ** -0.5, 0.1875, ((0, 16), (1, 2)), jnp.float32)
    w_down = bell_draw(splits[10], (FF, D), FF ** -0.5, 0.09375, ((0, 2), (1, 16)), jnp.float32)
    return {"token_ids": token_ids, "token_table": token_table, "row_table": row_table, "col_table": col_table, "chan_table": chan_table, "w_query": w_query, "w_key": w_key, "w_value": w_value, "w_out": w_out, "w_in": w_in, "w_down": w_down}


def layer_norm(values):
    center = values - lax.optimization_barrier(jnp.mean(values, axis=-1, keepdims=True))
    spread = lax.optimization_barrier(jnp.mean(center * center, axis=-1, keepdims=True))
    return center * lax.rsqrt(spread + 1e-05)

def embed(ids, where, token_table, row_table, col_table, chan_table):
    channel = where % 3
    pixel = where // 3
    image_row = pixel // IMG
    image_col = pixel % IMG
    summed = jnp.take(token_table, ids, axis=0) + jnp.take(row_table, image_row, axis=0)
    summed = summed + jnp.take(col_table, image_col, axis=0) + jnp.take(chan_table, channel, axis=0)
    return layer_norm(summed)

def reference(token_ids, token_table, row_table, col_table, chan_table, w_query, w_key, w_value, w_out, w_in, w_down):
    highest = lax.Precision.HIGHEST
    total = token_ids.shape[0]
    key_block = min(512, POS_DEV)
    lat_pos = (total - LAT + jnp.arange(LAT)).astype(jnp.int32)
    lat_emb = embed(token_ids[total - LAT:], lat_pos, token_table, row_table, col_table, chan_table)
    queries = jnp.dot(lat_emb, w_query, precision=highest).reshape(LAT, HEADS, HD).transpose(1, 0, 2) * HD ** (-0.5)

    def step(carry, start):
        top, weight, accum = carry
        where = (start + jnp.arange(key_block)).astype(jnp.int32)
        ids = lax.dynamic_slice_in_dim(token_ids, start, key_block)
        emb = embed(ids, where, token_table, row_table, col_table, chan_table)
        keys = jnp.dot(emb, w_key, precision=highest).reshape(key_block, HEADS, HD)
        vals = jnp.dot(emb, w_value, precision=highest).reshape(key_block, HEADS, HD)
        scores = jnp.einsum('hld,khd->hlk', queries, keys, precision=highest)
        scores = jnp.where(where[None, None, :] <= lat_pos[None, :, None], scores, -1e+30)
        new_top = jnp.maximum(top, lax.optimization_barrier(jnp.max(scores, axis=-1)))
        factor = jnp.exp(top - new_top)
        probs = jnp.exp(scores - new_top[..., None])
        weight = weight * factor + lax.optimization_barrier(jnp.sum(probs, axis=-1))
        accum = accum * factor[..., None] + jnp.einsum('hlk,khd->hld', probs, vals, precision=highest)
        return ((new_top, weight, accum), None)
    starts = (jnp.arange(total // key_block) * key_block).astype(jnp.int32)
    init = (jnp.full((HEADS, LAT), -1e+30, jnp.float32), jnp.zeros((HEADS, LAT), jnp.float32), jnp.zeros((HEADS, LAT, HD), jnp.float32))
    (top, weight, accum), _ = lax.scan(step, init, starts)
    attended = (accum / weight[..., None]).transpose(1, 0, 2).reshape(LAT, HEADS * HD)
    projected = jnp.dot(attended, w_out, precision=highest)
    hidden = jax.nn.gelu(jnp.dot(layer_norm(projected), w_in, precision=highest))
    return projected + jnp.dot(hidden, w_down, precision=highest)
```

```python
import functools

import jax
import jax.numpy as jnp
from jax import lax
from jax.experimental import pallas as pl
from jax.experimental.pallas import tpu as pltpu
from jax.sharding import PartitionSpec as P

HD = 64
IMG = 256
LAT = 512
LOG2E = 1.4426950408889634
ROWS_KEY = 16
ROWS_LAT = 8
EXTRA = 128
NARROW = jnp.bfloat16


def halves(x):
    high = x.astype(NARROW)
    return high, (x - high.astype(jnp.float32)).astype(NARROW)


def mm(a, b, dims=(((1,), (0,)), ((), ()))):
    return lax.dot_general(a, b, dims, preferred_element_type=jnp.float32)


def one_hot_t(info, lanes):
    tall = lax.broadcasted_iota(jnp.int32, (IMG, lanes), 0)
    short = lax.broadcasted_iota(jnp.int32, (EXTRA, lanes), 0)
    tok = jnp.where(tall == info[0:1], 1.0, 0.0).astype(NARROW)
    col = jnp.where(tall == info[1:2], 1.0, 0.0).astype(NARROW)
    pair = jnp.where((short == info[2:3]) | (short == info[3:4]), 1.0, 0.0).astype(NARROW)
    return jnp.concatenate([tok, col, pair], axis=0)


def spread_kernel(info_ref, tabs_ref, out_ref):
    lanes = info_ref.shape[1]
    pick = one_hot_t(info_ref[...], lanes)
    total = jnp.zeros((1, lanes), jnp.float32)
    depth = tabs_ref.shape[1]
    step = 256
    for at in range(0, depth, step):
        high, low = halves(tabs_ref[:, at : at + step])
        emb = mm(high, pick, (((0,), (0,)), ((), ()))) + mm(low, pick, (((0,), (0,)), ((), ())))
        total = total + jnp.sum(emb * emb, axis=0, keepdims=True)
    out_ref[...] = lax.rsqrt(total * (1.0 / depth) + 1e-05)


def attend_kernel(
    block, first_masked, info_ref, inv_ref, linfo_ref, linv_ref, tabs_ref, w_ref, flag_ref,
    out_ref, acc_ref, top_ref, kv_ref, q_ref,
):
    span = info_ref.shape[1]
    w_high, w_low = halves(w_ref[...])
    t_high, t_low = halves(tabs_ref[...])
    table = mm(t_high, w_high) + mm(t_high, w_low) + mm(t_low, w_high)
    table_t = table.T
    kv_high, kv_low = halves(table_t[0 : 2 * HD])
    kv_ref[...] = jnp.concatenate([kv_high, kv_low], axis=0)
    q_high, q_low = halves(table_t[2 * HD : 3 * HD])
    lat_pick = one_hot_t(linfo_ref[...], LAT)
    q_t = mm(q_high, lat_pick) + mm(q_low, lat_pick)
    q = (q_t * linv_ref[...] * (HD**-0.5 * LOG2E)).T
    q_high, q_low = halves(q)
    q_ref[...] = jnp.concatenate([q_high, q_high, q_low, q_low], axis=1)

    top_ref[...] = jnp.full(top_ref.shape, -1e30, jnp.float32)
    acc_ref[...] = jnp.zeros(acc_ref.shape, jnp.float32)

    def step(i, masked):
        at = pl.multiple_of(i * block, block)
        picked = mm(kv_ref[...], one_hot_t(info_ref[:, pl.ds(at, block)], block))
        both = (picked[0 : 2 * HD] + picked[2 * HD : 4 * HD]) * inv_ref[:, pl.ds(at, block)]
        high, low = halves(both)
        keys = jnp.concatenate([high[:HD], low[:HD], high[:HD], low[:HD]], axis=0)
        vals = jnp.concatenate(
            [high[HD:], low[HD:], jnp.ones((2 * HD, block), NARROW)], axis=0
        )
        scores = mm(q_ref[...], keys)
        if masked:
            back = span - at
            lane = lax.broadcasted_iota(jnp.int32, (LAT, block), 1) - back + LAT
            lat = lax.broadcasted_iota(jnp.int32, (LAT, block), 0)
            scores = jnp.where(lane <= lat, scores, -1e30)
        old = top_ref[:, 0:1]
        new = jnp.maximum(old, jnp.max(scores, axis=1, keepdims=True))
        probs = jnp.exp2(scores - new)
        p_high, p_low = halves(probs)
        dims = (((1,), (1,)), ((), ()))
        acc_ref[...] = acc_ref[...] * jnp.exp2(old - new) + (
            mm(p_high, vals, dims) + mm(p_low, vals, dims)
        )
        top_ref[...] = jnp.broadcast_to(new, top_ref.shape)

    last = flag_ref[0] == 1

    def body(i, carry):
        hide = last & (i >= first_masked)

        @pl.when(hide)
        def _():
            step(i, True)

        @pl.when(jnp.logical_not(hide))
        def _():
            step(i, False)

        return carry

    lax.fori_loop(0, span // block, body, 0)
    acc = acc_ref[...]
    out_ref[...] = jnp.concatenate(
        [acc[:, :HD] + acc[:, HD : 2 * HD], acc[:, 2 * HD : 2 * HD + 32], top_ref[:, 0:32]],
        axis=1,
    )


def layer_norm(values):
    center = values - jnp.mean(values, axis=-1, keepdims=True)
    spread = jnp.mean(center * center, axis=-1, keepdims=True)
    return center * lax.rsqrt(spread + 1e-05)


def describe(ids, where, row_at, row_first, chan_at):
    pixel = where // 3
    return jnp.stack(
        [ids, pixel % IMG, pixel // IMG - row_first + row_at, where % 3 + chan_at]
        + [jnp.zeros_like(ids)] * 4
    )


def per_device(
    token_ids,
    token_table,
    row_table,
    col_table,
    chan_table,
    w_query,
    w_key,
    w_value,
    w_out,
    w_in,
    w_down,
):
    high = lax.Precision.HIGH
    local = token_ids.shape[0]
    n_pos = lax.axis_size("pos")
    index = lax.axis_index("pos")
    total = local * n_pos
    heads_dev = w_key.shape[1] // HD
    parts = n_pos // heads_dev
    span = total // parts
    head, part = index // parts, index % parts
    depth = token_table.shape[1]

    def centered(table):
        return table - jnp.mean(table, axis=-1, keepdims=True)

    row_mid = centered(row_table)

    def rows_from(start, count):
        first = jnp.minimum(start // 3 // IMG, row_table.shape[0] - count)
        return first, lax.dynamic_slice_in_dim(row_mid, first, count)

    own_first, own_rows = rows_from(index * local, ROWS_KEY)
    key_first, key_rows = rows_from(part * span, ROWS_KEY)
    lat_first, lat_rows_tab = rows_from(jnp.int32(total - LAT), ROWS_LAT)
    base = [centered(token_table), centered(col_table)]
    tail = [
        lat_rows_tab,
        centered(chan_table),
        jnp.zeros((EXTRA - ROWS_KEY - ROWS_LAT - 3, depth), jnp.float32),
    ]
    own_tabs = jnp.concatenate(base + [own_rows] + tail)
    tabs = jnp.concatenate(base + [key_rows] + tail)
    chan_at = ROWS_KEY + ROWS_LAT

    own_where = index * local + jnp.arange(local, dtype=jnp.int32)
    own_info = describe(token_ids, own_where, 0, own_first, chan_at)
    inv = pl.pallas_call(
        spread_kernel,
        out_shape=jax.ShapeDtypeStruct((1, local), jnp.float32),
        compiler_params=pltpu.CompilerParams(vmem_limit_bytes=48 * 2**20),
    )(own_info, own_tabs)

    sent = jnp.concatenate([token_ids.astype(jnp.float32)[None], inv])
    got = lax.all_gather(sent, "pos", axis=1, tiled=True)
    all_ids = got[0].astype(jnp.int32)
    key_ids = lax.dynamic_slice_in_dim(all_ids, part * span, span)
    key_inv = lax.dynamic_slice_in_dim(got[1:2], part * span, span, axis=1)
    key_where = part * span + jnp.arange(span, dtype=jnp.int32)
    key_info = describe(key_ids, key_where, 0, key_first, chan_at)
    lat_where = total - LAT + jnp.arange(LAT, dtype=jnp.int32)
    lat_info = describe(all_ids[total - LAT :], lat_where, ROWS_KEY, lat_first, chan_at)
    lat_inv = got[1:2, total - LAT :]

    def of_head(w):
        return lax.dynamic_slice_in_dim(w, head * HD, HD, axis=1)

    w_qkv = jnp.concatenate(
        [of_head(w_key), of_head(w_value), of_head(w_query), jnp.zeros((depth, HD), jnp.float32)],
        axis=1,
    )
    block = min(1024, span)
    first_masked = (span - LAT) // block
    flag = (part == parts - 1).astype(jnp.int32)[None]
    vmem = pl.BlockSpec(memory_space=pltpu.VMEM)
    state = pl.pallas_call(
        functools.partial(attend_kernel, block, first_masked),
        out_shape=jax.ShapeDtypeStruct((LAT, 2 * HD), jnp.float32),
        in_specs=[vmem] * 6 + [pl.BlockSpec(memory_space=pltpu.SMEM)],
        out_specs=vmem,
        scratch_shapes=[
            pltpu.VMEM((LAT, 4 * HD), jnp.float32),
            pltpu.VMEM((LAT, 128), jnp.float32),
            pltpu.VMEM((4 * HD, 2 * IMG + EXTRA), NARROW),
            pltpu.VMEM((LAT, 4 * HD), NARROW),
        ],
        compiler_params=pltpu.CompilerParams(vmem_limit_bytes=48 * 2**20),
        cost_estimate=pl.CostEstimate(
            flops=20 * 10**9, bytes_accessed=8 * 2**20, transcendentals=4 * 2**20
        ),
    )(key_info, key_inv, lat_info, lat_inv, tabs, w_qkv, flag)

    whole_out = lax.all_gather(w_out, "pos", axis=1, tiled=True)
    my_in = lax.all_to_all(w_in, "pos", split_axis=1, concat_axis=0, tiled=True)
    my_down = lax.all_to_all(w_down, "pos", split_axis=0, concat_axis=1, tiled=True)

    lat_rows = LAT // n_pos
    states = lax.all_to_all(state, "pos", split_axis=0, concat_axis=0, tiled=True)
    states = states.reshape(heads_dev, parts, lat_rows, 2 * HD)
    tops = states[..., 96:97]
    factor = jnp.exp2(tops - jnp.max(tops, axis=1, keepdims=True))
    weight = jnp.sum(states[..., 64:65] * factor, axis=1)
    accum = jnp.sum(states[..., :HD] * factor, axis=1)
    attended = (accum / weight).transpose(1, 0, 2).reshape(lat_rows, heads_dev * HD)
    projected = lax.psum(jnp.dot(attended, whole_out, precision=high), "head")
    normed = lax.all_gather(layer_norm(projected), "pos", axis=0, tiled=True)
    hidden = jax.nn.gelu(jnp.dot(normed, my_in, precision=high))
    down = jnp.dot(hidden, my_down, precision=high)
    down = lax.psum_scatter(down, "pos", scatter_dimension=0, tiled=True)
    return projected + lax.psum(down, "head")


def solution(mesh):
    placed = (
        P("pos"),
        P(),
        P(),
        P(),
        P(),
        P(None, "head"),
        P(None, "head"),
        P(None, "head"),
        P("head", "pos"),
        P("pos", "head"),
        P("head", "pos"),
    )
    return jax.shard_map(
        per_device, mesh=mesh, in_specs=placed, out_specs=P("pos", None), check_vma=False
    )
```

```python
import functools

import jax
import jax.numpy as jnp
from jax import lax
from jax.experimental import pallas as pl
from jax.experimental.pallas import tpu as pltpu
from jax.sharding import PartitionSpec as P

HD = 64
IMG = 256
LAT = 512
LOG2E = 1.4426950408889634
ROWS_KEY = 16
ROWS_LAT = 8
EXTRA = 128
NARROW = jnp.bfloat16


def halves(x):
    high = x.astype(NARROW)
    return high, (x - high.astype(jnp.float32)).astype(NARROW)


def mm(a, b, dims=(((1,), (0,)), ((), ()))):
    return lax.dot_general(a, b, dims, preferred_element_type=jnp.float32)


def mm3(a, b, dims=(((1,), (0,)), ((), ()))):
    a_high, a_low = halves(a)
    b_high, b_low = halves(b)
    return mm(a_high, b_high, dims) + (mm(a_high, b_low, dims) + mm(a_low, b_high, dims))


def send(src, dst, sems, at, pos, head):
    copy = pltpu.make_async_remote_copy(
        src_ref=src,
        dst_ref=dst,
        send_sem=sems[0].at[at],
        recv_sem=sems[1].at[at],
        device_id={"pos": pos, "head": head},
        device_id_type=pl.DeviceIdType.MESH,
    )
    copy.start()
    return copy


def greet(partners):
    barrier = pltpu.get_barrier_semaphore()
    for pos, head in partners:
        pl.semaphore_signal(
            barrier,
            inc=1,
            device_id={"pos": pos, "head": head},
            device_id_type=pl.DeviceIdType.MESH,
        )
    pl.semaphore_wait(barrier, len(partners))


def share_kernel(n_pos, own_ref, all_ref, got, send_sem, recv_sem):
    me, head = lax.axis_index("pos"), lax.axis_index("head")
    peers = [(lax.rem(me + k, n_pos), head) for k in range(1, n_pos)]
    greet(peers)
    copies = []
    for k, (peer, _) in enumerate(peers):
        copies.append(send(own_ref, got.at[me], (send_sem, recv_sem), k, peer, head))
    got[me] = own_ref[...]
    for copy in copies:
        copy.wait()
    all_ref[...] = got[...]


def one_hot_t(info, lanes):
    tall = lax.broadcasted_iota(jnp.int32, (IMG, lanes), 0)
    short = lax.broadcasted_iota(jnp.int32, (EXTRA, lanes), 0)
    tok = jnp.where(tall == info[0:1], 1.0, 0.0).astype(NARROW)
    col = jnp.where(tall == info[1:2], 1.0, 0.0).astype(NARROW)
    pair = jnp.where((short == info[2:3]) | (short == info[3:4]), 1.0, 0.0).astype(NARROW)
    return jnp.concatenate([tok, col, pair], axis=0)


def spread_kernel(info_ref, tabs_ref, out_ref):
    lanes = info_ref.shape[1]
    pick = one_hot_t(info_ref[...], lanes)
    total = jnp.zeros((1, lanes), jnp.float32)
    depth = tabs_ref.shape[1]
    step = 256
    for at in range(0, depth, step):
        high, low = halves(tabs_ref[:, at : at + step])
        emb = mm(high, pick, (((0,), (0,)), ((), ()))) + mm(low, pick, (((0,), (0,)), ((), ())))
        total = total + jnp.sum(emb * emb, axis=0, keepdims=True)
    out_ref[...] = lax.rsqrt(total * (1.0 / depth) + 1e-05)


def attend_kernel(
    block, first_masked, n_pos, parts, moves, info_ref, inv_ref, linfo_ref, linv_ref, tabs_ref,
    w_ref, mlp_ref, out_ref, mlp_out_ref, acc_ref, top_ref, kv_ref, q_ref, state_ref, got_ref,
    mlp_send, mlp_recv, own_sem, st_send, st_recv,
):
    me, head = lax.axis_index("pos"), lax.axis_index("head")
    peers = [lax.rem(me + k, n_pos) for k in range(1, n_pos)]
    greet([(peer, head) for peer in peers])
    copies = []
    if moves:
        wide = mlp_ref.shape[1] // n_pos

        def slab(peer):
            return mlp_ref.at[:, pl.ds(pl.multiple_of(peer * wide, wide), wide)]

        for k, peer in enumerate(peers):
            copies.append(
                send(slab(peer), mlp_out_ref.at[me], (mlp_send, mlp_recv), k, peer, head)
            )
        own = pltpu.make_async_copy(slab(me), mlp_out_ref.at[me], own_sem)
        own.start()
        copies.append(own)

    span = info_ref.shape[1]
    w_high, w_low = halves(w_ref[...])
    t_high, t_low = halves(tabs_ref[...])
    table = mm(t_high, w_high) + mm(t_high, w_low) + mm(t_low, w_high)
    table_t = table.T
    kv_high, kv_low = halves(table_t[0 : 2 * HD])
    kv_ref[...] = jnp.concatenate([kv_high, kv_low], axis=0)
    q_high, q_low = halves(table_t[2 * HD : 3 * HD])
    lat_pick = one_hot_t(linfo_ref[...], LAT)
    q_t = mm(q_high, lat_pick) + mm(q_low, lat_pick)
    q = (q_t * linv_ref[...] * (HD**-0.5 * LOG2E)).T
    q_high, q_low = halves(q)
    q_ref[...] = jnp.concatenate([q_high, q_high, q_low, q_low], axis=1)

    top_ref[...] = jnp.full(top_ref.shape, -1e30, jnp.float32)
    acc_ref[...] = jnp.zeros(acc_ref.shape, jnp.float32)

    def step(i, masked):
        at = pl.multiple_of(i * block, block)
        picked = mm(kv_ref[...], one_hot_t(info_ref[:, pl.ds(at, block)], block))
        both = (picked[0 : 2 * HD] + picked[2 * HD : 4 * HD]) * inv_ref[:, pl.ds(at, block)]
        high, low = halves(both)
        keys = jnp.concatenate([high[:HD], low[:HD], high[:HD], low[:HD]], axis=0)
        vals = jnp.concatenate(
            [high[HD:], low[HD:], jnp.ones((2 * HD, block), NARROW)], axis=0
        )
        scores = mm(q_ref[...], keys)
        if masked:
            back = span - at
            lane = lax.broadcasted_iota(jnp.int32, (LAT, block), 1) - back + LAT
            lat = lax.broadcasted_iota(jnp.int32, (LAT, block), 0)
            scores = jnp.where(lane <= lat, scores, -1e30)
        old = top_ref[:, 0:1]
        new = jnp.maximum(old, jnp.max(scores, axis=1, keepdims=True))
        probs = jnp.exp2(scores - new)
        p_high, p_low = halves(probs)
        dims = (((1,), (1,)), ((), ()))
        acc_ref[...] = acc_ref[...] * jnp.exp2(old - new) + (
            mm(p_high, vals, dims) + mm(p_low, vals, dims)
        )
        top_ref[...] = jnp.broadcast_to(new, top_ref.shape)

    last = lax.rem(me, parts) == parts - 1

    def body(i, carry):
        hide = last & (i >= first_masked)

        @pl.when(hide)
        def _():
            step(i, True)

        @pl.when(jnp.logical_not(hide))
        def _():
            step(i, False)

        return carry

    lax.fori_loop(0, span // block, body, 0)
    acc = acc_ref[...]
    state_ref[...] = jnp.concatenate(
        [acc[:, :HD] + acc[:, HD : 2 * HD], acc[:, 2 * HD : 2 * HD + 32], top_ref[:, 0:32]],
        axis=1,
    )
    rows = LAT // n_pos

    def latents_of(peer):
        return pl.ds(pl.multiple_of(peer * rows, rows), rows)

    for k, peer in enumerate(peers):
        copies.append(
            send(state_ref.at[latents_of(peer)], got_ref.at[me], (st_send, st_recv), k, peer, head)
        )
    got_ref[me] = state_ref[latents_of(me), :]
    for copy in copies:
        copy.wait()
    out_ref[...] = got_ref[...]


def mlp_kernel(
    n_pos, heads, outer, part_ref, in_ref, down_ref, out_ref,
    sums, lanes, full, other, other_got, red, red_got, mid, mid_got, last,
    s0, r0, s1, r1, s2, r2, s3, r3, s4, r4, s5, r5, s6, r6, s7, r7,
):
    inner = n_pos // outer
    me, head = lax.axis_index("pos"), lax.axis_index("head")
    z, s = me // inner, lax.rem(me, inner)
    cols = full.shape[-1]
    lat = n_pos * full.shape[3]
    siblings = [lax.rem(head + k, heads) for k in range(1, heads)]
    deep = [lax.rem(z + k, outer) for k in range(1, outer)]
    flat = [lax.rem(s + k, inner) for k in range(1, inner)]
    greet(
        [(me, h) for h in siblings]
        + [(zz * inner + s, head) for zz in deep]
        + [(z * inner + ss, head) for ss in flat]
    )

    sums[head] = part_ref[...]
    copies = [
        send(sums.at[head], sums.at[head], (s0, r0), k, me, h) for k, h in enumerate(siblings)
    ]
    for copy in copies:
        copy.wait()
    projected = sums[0]
    for h in range(1, heads):
        projected = projected + sums[h]
    normed = layer_norm(projected)
    for h in range(heads):
        lanes[h] = normed[:, h * cols : (h + 1) * cols]
    full[head, z, s] = lanes[head]

    mine = full.at[head, z, s]
    copies = [
        send(mine, mine, (s1, r1), k, zz * inner + s, head) for k, zz in enumerate(deep)
    ]
    for copy in copies:
        copy.wait()
    mine = full.at[head, :, s]
    copies = [
        send(mine, mine, (s2, r2), k, z * inner + ss, head) for k, ss in enumerate(flat)
    ]
    across = [
        send(mine, mine, (s3, r3), k * inner, me, h) for k, h in enumerate(siblings)
    ]
    for j, copy in enumerate(copies):
        copy.wait()
        came = full.at[head, :, lax.rem(s - (j + 1) + inner, inner)]
        across += [
            send(came, came, (s3, r3), k * inner + j + 1, me, h)
            for k, h in enumerate(siblings)
        ]

    def weights(h):
        return pl.ds(pl.multiple_of(h * cols, cols), cols)

    def hidden_from(h):
        return mm3(full[h].reshape(lat, cols), in_ref[weights(h), :])

    hidden = hidden_from(head)
    for copy in across:
        copy.wait()
    for h in siblings:
        hidden = hidden + hidden_from(h)
    cube = hidden * hidden * hidden
    hidden = 0.5 * hidden * (1.0 + jnp.tanh(0.7978845608028654 * (hidden + 0.044715 * cube)))

    def down_to(h):
        return mm3(hidden, down_ref[weights(h), :], (((1,), (1,)), ((), ())))

    copies = []
    for k, h in enumerate(siblings):
        other[k] = down_to(h)
        copies.append(send(other.at[k], other_got.at[k], (s4, r4), k, me, h))
    total = down_to(head)
    for k, copy in enumerate(copies):
        copy.wait()
        total = total + other_got[k]
    red[...] = total.reshape(red.shape)

    copies = [
        send(red.at[:, ss], red_got.at[k], (s5, r5), k, z * inner + ss, head)
        for k, ss in enumerate(flat)
    ]
    total = red[:, s]
    for k, copy in enumerate(copies):
        copy.wait()
        total = total + red_got[k]
    mid[...] = total
    copies = [
        send(mid.at[zz], mid_got.at[k], (s6, r6), k, zz * inner + s, head)
        for k, zz in enumerate(deep)
    ]
    total = mid[z]
    for k, copy in enumerate(copies):
        copy.wait()
        total = total + mid_got[k]
    last[head] = total
    copies = [
        send(last.at[head], last.at[head], (s7, r7), k, me, h) for k, h in enumerate(siblings)
    ]
    for copy in copies:
        copy.wait()
    out_ref[...] = projected + jnp.concatenate([last[h] for h in range(heads)], axis=1)


def layer_norm(values):
    center = values - jnp.mean(values, axis=-1, keepdims=True)
    spread = jnp.mean(center * center, axis=-1, keepdims=True)
    return center * lax.rsqrt(spread + 1e-05)


def describe(ids, where, row_at, row_first, chan_at):
    pixel = where // 3
    return jnp.stack(
        [ids, pixel % IMG, pixel // IMG - row_first + row_at, where % 3 + chan_at]
        + [jnp.zeros_like(ids)] * 4
    )


def per_device(
    token_ids,
    token_table,
    row_table,
    col_table,
    chan_table,
    w_query,
    w_key,
    w_value,
    w_out,
    w_in,
    w_down,
):
    high = lax.Precision.HIGH
    local = token_ids.shape[0]
    n_pos = lax.axis_size("pos")
    index = lax.axis_index("pos")
    total = local * n_pos
    heads_dev = w_key.shape[1] // HD
    parts = n_pos // heads_dev
    span = total // parts
    head, part = index // parts, index % parts
    depth = token_table.shape[1]

    def centered(table):
        return table - jnp.mean(table, axis=-1, keepdims=True)

    row_mid = centered(row_table)

    def rows_from(start, count):
        first = jnp.minimum(start // 3 // IMG, row_table.shape[0] - count)
        return first, lax.dynamic_slice_in_dim(row_mid, first, count)

    own_first, own_rows = rows_from(index * local, ROWS_KEY)
    key_first, key_rows = rows_from(part * span, ROWS_KEY)
    lat_first, lat_rows_tab = rows_from(jnp.int32(total - LAT), ROWS_LAT)
    base = [centered(token_table), centered(col_table)]
    tail = [
        lat_rows_tab,
        centered(chan_table),
        jnp.zeros((EXTRA - ROWS_KEY - ROWS_LAT - 3, depth), jnp.float32),
    ]
    own_tabs = jnp.concatenate(base + [own_rows] + tail)
    tabs = jnp.concatenate(base + [key_rows] + tail)
    chan_at = ROWS_KEY + ROWS_LAT

    own_where = index * local + jnp.arange(local, dtype=jnp.int32)
    own_info = describe(token_ids, own_where, 0, own_first, chan_at)
    inv = pl.pallas_call(
        spread_kernel,
        out_shape=jax.ShapeDtypeStruct((1, local), jnp.float32),
        compiler_params=pltpu.CompilerParams(vmem_limit_bytes=48 * 2**20),
    )(own_info, own_tabs)

    vmem = pl.BlockSpec(memory_space=pltpu.VMEM)
    hbm = pl.BlockSpec(memory_space=pl.ANY)
    dma = pltpu.SemaphoreType.DMA
    sent = jnp.concatenate(
        [token_ids.astype(jnp.float32).reshape(-1, 128), inv.reshape(-1, 128)]
    )
    got = pl.pallas_call(
        functools.partial(share_kernel, n_pos),
        out_shape=jax.ShapeDtypeStruct((n_pos,) + sent.shape, jnp.float32),
        in_specs=[vmem],
        out_specs=vmem,
        scratch_shapes=[
            pltpu.VMEM((n_pos,) + sent.shape, jnp.float32),
            dma((n_pos - 1,)),
            dma((n_pos - 1,)),
        ],
        compiler_params=pltpu.CompilerParams(collective_id=0, has_side_effects=True),
    )(sent)
    got = got.reshape(n_pos, 2, local).transpose(1, 0, 2).reshape(2, total)
    all_ids = got[0].astype(jnp.int32)
    key_ids = lax.dynamic_slice_in_dim(all_ids, part * span, span)
    key_inv = lax.dynamic_slice_in_dim(got[1:2], part * span, span, axis=1)
    key_where = part * span + jnp.arange(span, dtype=jnp.int32)
    key_info = describe(key_ids, key_where, 0, key_first, chan_at)
    lat_where = total - LAT + jnp.arange(LAT, dtype=jnp.int32)
    lat_info = describe(all_ids[total - LAT :], lat_where, ROWS_KEY, lat_first, chan_at)
    lat_inv = got[1:2, total - LAT :]

    def of_head(w):
        return lax.dynamic_slice_in_dim(w, head * HD, HD, axis=1)

    w_qkv = jnp.concatenate(
        [of_head(w_key), of_head(w_value), of_head(w_query), jnp.zeros((depth, HD), jnp.float32)],
        axis=1,
    )
    block = min(1024, span)
    first_masked = (span - LAT) // block
    ff_rows = w_in.shape[1] // n_pos
    lat_rows = LAT // n_pos
    moves = ff_rows % 128 == 0
    mlp_weights = jnp.concatenate([w_in, w_down.T])
    if not moves:
        mlp_kept = lax.all_to_all(
            mlp_weights.reshape(-1, n_pos, ff_rows).transpose(1, 0, 2),
            "pos", split_axis=0, concat_axis=0, tiled=True,
        )
        mlp_weights = jnp.zeros((8, 128), jnp.float32)
    mlp_shape = (n_pos, mlp_weights.shape[0], ff_rows) if moves else (8, 128)
    state_shape = (n_pos, lat_rows, 2 * HD)
    states, mlp_moved = pl.pallas_call(
        functools.partial(attend_kernel, block, first_masked, n_pos, parts, moves),
        out_shape=[
            jax.ShapeDtypeStruct(state_shape, jnp.float32),
            jax.ShapeDtypeStruct(mlp_shape, jnp.float32),
        ],
        in_specs=[vmem] * 6 + [hbm],
        out_specs=[vmem, hbm],
        scratch_shapes=[
            pltpu.VMEM((LAT, 4 * HD), jnp.float32),
            pltpu.VMEM((LAT, 128), jnp.float32),
            pltpu.VMEM((4 * HD, 2 * IMG + EXTRA), NARROW),
            pltpu.VMEM((LAT, 4 * HD), NARROW),
            pltpu.VMEM((LAT, 2 * HD), jnp.float32),
            pltpu.VMEM(state_shape, jnp.float32),
            dma((n_pos - 1,)),
            dma((n_pos - 1,)),
            dma,
            dma((n_pos - 1,)),
            dma((n_pos - 1,)),
        ],
        compiler_params=pltpu.CompilerParams(
            vmem_limit_bytes=48 * 2**20, collective_id=1, has_side_effects=True
        ),
        cost_estimate=pl.CostEstimate(
            flops=20 * 10**9, bytes_accessed=8 * 2**20, transcendentals=4 * 2**20
        ),
    )(key_info, key_inv, lat_info, lat_inv, tabs, w_qkv, mlp_weights)
    if moves:
        mlp_kept = mlp_moved
    in_rows = w_in.shape[0]
    my_in = mlp_kept[:, :in_rows].reshape(-1, ff_rows)
    my_down = mlp_kept[:, in_rows:].reshape(-1, ff_rows)

    whole_out = lax.all_gather(w_out, "pos", axis=1, tiled=True)
    states = states.reshape(heads_dev, parts, lat_rows, 2 * HD)
    tops = states[..., 96:97]
    factor = jnp.exp2(tops - jnp.max(tops, axis=1, keepdims=True))
    weight = jnp.sum(states[..., 64:65] * factor, axis=1)
    accum = jnp.sum(states[..., :HD] * factor, axis=1)
    attended = (accum / weight).transpose(1, 0, 2).reshape(lat_rows, heads_dev * HD)
    partial_out = jnp.dot(attended, whole_out, precision=high)

    heads = lax.axis_size("head")
    outer = 4 if n_pos % 4 == 0 else 1
    inner = n_pos // outer
    cols = depth // heads

    def room(*shape):
        return pltpu.VMEM(shape, jnp.float32)

    counts = [heads, outer, inner, heads * inner, heads, inner, outer, heads]
    return pl.pallas_call(
        functools.partial(mlp_kernel, n_pos, heads, outer),
        out_shape=jax.ShapeDtypeStruct((lat_rows, depth), jnp.float32),
        in_specs=[vmem] * 3,
        out_specs=vmem,
        scratch_shapes=[
            room(heads, lat_rows, depth),
            room(heads, lat_rows, cols),
            room(heads, outer, inner, lat_rows, cols),
            room(heads - 1, LAT, cols),
            room(heads - 1, LAT, cols),
            room(outer, inner, lat_rows, cols),
            room(inner - 1, outer, lat_rows, cols),
            room(outer, lat_rows, cols),
            room(outer - 1, lat_rows, cols),
            room(heads, lat_rows, cols),
        ]
        + [dma((count,)) for count in counts for _ in range(2)],
        compiler_params=pltpu.CompilerParams(
            vmem_limit_bytes=48 * 2**20, collective_id=2, has_side_effects=True
        ),
    )(partial_out, my_in, my_down)


def solution(mesh):
    placed = (
        P("pos"),
        P(),
        P(),
        P(),
        P(),
        P(None, "head"),
        P(None, "head"),
        P(None, "head"),
        P("head", "pos"),
        P("pos", "head"),
        P("head", "pos"),
    )
    return jax.shard_map(
        per_device, mesh=mesh, in_specs=placed, out_specs=P("pos", None), check_vma=False
    )
```

```python
import functools

import jax
import jax.numpy as jnp
from jax import lax
from jax.experimental import pallas as pl
from jax.experimental.pallas import tpu as pltpu
from jax.sharding import PartitionSpec as P

HD = 64
IMG = 256
LAT = 512
LOG2E = 1.4426950408889634
ROWS_KEY = 24
ROWS_OWN = 16
ROWS_LAT = 16
CHAN_AT = ROWS_KEY + ROWS_OWN + ROWS_LAT
EXTRA = 128
NARROW = jnp.bfloat16


def halves(x):
    high = x.astype(NARROW)
    return high, (x - high.astype(jnp.float32)).astype(NARROW)


def mm(a, b, dims=(((1,), (0,)), ((), ()))):
    return lax.dot_general(a, b, dims, preferred_element_type=jnp.float32)


def mm3(a, b, dims=(((1,), (0,)), ((), ()))):
    a_high, a_low = halves(a)
    b_high, b_low = halves(b)
    return mm(a_high, b_high, dims) + (mm(a_high, b_low, dims) + mm(a_low, b_high, dims))


def send(src, dst, sems, at, pos, head):
    copy = pltpu.make_async_remote_copy(
        src_ref=src,
        dst_ref=dst,
        send_sem=sems[0].at[at],
        recv_sem=sems[1].at[at],
        device_id={"pos": pos, "head": head},
        device_id_type=pl.DeviceIdType.MESH,
    )
    copy.start()
    return copy


def greet(partners):
    barrier = pltpu.get_barrier_semaphore()
    for pos, head in partners:
        pl.semaphore_signal(
            barrier,
            inc=1,
            device_id={"pos": pos, "head": head},
            device_id_type=pl.DeviceIdType.MESH,
        )
    pl.semaphore_wait(barrier, len(partners))


def one_hot_t(ids, where, row_first, row_at):
    lanes = ids.shape[1]
    pixel = jnp.floor((where.astype(jnp.float32) + 0.5) * (1.0 / 3.0)).astype(jnp.int32)
    chan = where - 3 * pixel + CHAN_AT
    row = (pixel >> 8) - row_first + row_at
    column = pixel & (IMG - 1)
    tall = lax.broadcasted_iota(jnp.int32, (IMG, lanes), 0)
    short = lax.broadcasted_iota(jnp.int32, (EXTRA, lanes), 0)
    tok = jnp.where(tall == ids, 1.0, 0.0).astype(NARROW)
    col = jnp.where(tall == column, 1.0, 0.0).astype(NARROW)
    pair = jnp.where((short == row) | (short == chan), 1.0, 0.0).astype(NARROW)
    return jnp.concatenate([tok, col, pair], axis=0)


def front_kernel(
    n_pos, parts, outer, moves,
    ids_ref, tok_ref, row_ref, col_ref, chan_ref, wk_ref, wv_ref, wq_ref, wo_ref, mlp_ref,
    out_ref, wo_out_ref, mlp_out_ref,
    tabs_ref, high_ref, low_ref, w_ref, ids_got, acc_ref, top_ref, kv_ref, q_ref, state_ref,
    got_ref, w_sem, own_sem, id_send, id_recv, wz_send, wz_recv, wp_send, wp_recv,
    mlp_send, mlp_recv, st_send, st_recv,
):
    inner = n_pos // outer
    me, head = lax.axis_index("pos"), lax.axis_index("head")
    z, s = me // inner, lax.rem(me, inner)
    peers = [lax.rem(me + k, n_pos) for k in range(1, n_pos)]
    deep = [lax.rem(z + k, outer) for k in range(1, outer)]
    flat = [lax.rem(s + k, inner) for k in range(1, inner)]
    greet([(peer, head) for peer in peers])
    local = ids_ref.shape[1]
    total = local * n_pos
    span = total // parts
    slot, part = me // parts, lax.rem(me, parts)

    at = pl.multiple_of(slot // 2 * 2 * HD, 2 * HD)
    loads = []
    for k, ref in enumerate((wk_ref, wv_ref, wq_ref)):
        loads.append(
            pltpu.make_async_copy(ref.at[:, pl.ds(at, 2 * HD)], w_ref.at[k], w_sem.at[k])
        )
        loads[-1].start()

    def rows_from(start, count):
        first = start // (3 * IMG) // 8 * 8
        first = jnp.minimum(first, row_ref.shape[0] - count)
        return first, row_ref[pl.ds(pl.multiple_of(first, 8), count), :]

    key_first, key_rows = rows_from(part * span, ROWS_KEY)
    own_first, own_rows = rows_from(me * local, ROWS_OWN)
    lat_first, lat_rows = rows_from(jnp.int32(total - LAT), ROWS_LAT)
    tabs_ref[2 * IMG :, :] = jnp.zeros((EXTRA, tabs_ref.shape[1]), jnp.float32)
    tabs_ref[2 * IMG + CHAN_AT : 2 * IMG + CHAN_AT + 3, :] = chan_ref[...]
    extra = jnp.concatenate([key_rows, own_rows, lat_rows, tabs_ref[2 * IMG + CHAN_AT :, :]])
    for k, table in enumerate((tok_ref[...], col_ref[...], extra)):
        mid = table - jnp.mean(table, axis=1, keepdims=True)
        high, low = halves(mid)
        high_ref[k * IMG : k * IMG + table.shape[0], :] = high
        low_ref[k * IMG : k * IMG + table.shape[0], :] = low

    iota = lax.broadcasted_iota(jnp.int32, (1, local), 1)
    ids = ids_ref[...]
    pick = one_hot_t(ids, me * local + iota, own_first, ROWS_KEY)
    depth = tabs_ref.shape[1]
    square = jnp.zeros((1, local), jnp.float32)
    dims = (((0,), (0,)), ((), ()))
    for c in range(0, depth, 256):
        emb = mm(high_ref[:, c : c + 256], pick, dims) + mm(low_ref[:, c : c + 256], pick, dims)
        square = square + jnp.sum(emb * emb, axis=0, keepdims=True)
    inv = lax.rsqrt(square * (1.0 / depth) + 1e-05)
    ids_got[me] = jnp.concatenate([ids.astype(jnp.float32), inv], axis=0)
    id_copies = [
        send(ids_got.at[me], ids_got.at[me], (id_send, id_recv), k, peer, head)
        for k, peer in enumerate(peers)
    ]

    own = pltpu.make_async_copy(wo_ref, wo_out_ref.at[z, s], own_sem.at[0])
    own.start()
    wz_copies = [
        send(wo_ref, wo_out_ref.at[z, s], (wz_send, wz_recv), k, zz * inner + s, head)
        for k, zz in enumerate(deep)
    ]
    copies = []
    if moves:
        wide = mlp_ref.shape[1] // n_pos

        def slab(peer):
            return mlp_ref.at[:, pl.ds(pl.multiple_of(peer * wide, wide), wide)]

        for k, peer in enumerate(peers):
            copies.append(
                send(slab(peer), mlp_out_ref.at[me], (mlp_send, mlp_recv), k, peer, head)
            )
        kept = pltpu.make_async_copy(slab(me), mlp_out_ref.at[me], own_sem.at[1])
        kept.start()
        copies.append(kept)

    for load in loads:
        load.wait()
    even = lax.rem(slot, 2) == 0
    w = jnp.concatenate(
        [jnp.where(even, w_ref[k][:, :HD], w_ref[k][:, HD:]) for k in range(3)]
        + [jnp.zeros((depth, HD), jnp.float32)],
        axis=1,
    )
    w_high, w_low = halves(w)
    table = (
        mm(high_ref[...], w_high) + mm(high_ref[...], w_low) + mm(low_ref[...], w_high)
    )
    table_t = table.T
    kv_high, kv_low = halves(table_t[0 : 2 * HD])
    kv_ref[...] = jnp.concatenate([kv_high, kv_low], axis=0)
    q_high, q_low = halves(table_t[2 * HD : 3 * HD])
    top_ref[...] = jnp.full(top_ref.shape, -1e30, jnp.float32)
    acc_ref[...] = jnp.zeros(acc_ref.shape, jnp.float32)
    for copy in id_copies:
        copy.wait()

    late = ids_got[n_pos - 1][:, local - LAT :]
    lat_where = total - LAT + lax.broadcasted_iota(jnp.int32, (1, LAT), 1)
    lat_pick = one_hot_t(late[0:1].astype(jnp.int32), lat_where, lat_first, ROWS_KEY + ROWS_OWN)
    q_t = mm(q_high, lat_pick) + mm(q_low, lat_pick)
    q = (q_t * late[1:2] * (HD**-0.5 * LOG2E)).T
    q_high, q_low = halves(q)
    q_ref[...] = jnp.concatenate([q_high, q_high, q_low, q_low], axis=1)

    blocks = span // local
    last = part == parts - 1

    def step(i, masked=False):
        chunk = part * blocks + i
        got = ids_got[chunk]
        pick = one_hot_t(got[0:1].astype(jnp.int32), chunk * local + iota, key_first, 0)
        picked = mm(kv_ref[...], pick)
        both = (picked[0 : 2 * HD] + picked[2 * HD : 4 * HD]) * got[1:2]
        high, low = halves(both)
        keys = jnp.concatenate([high[:HD], low[:HD], high[:HD], low[:HD]], axis=0)
        vals = jnp.concatenate(
            [high[HD:], low[HD:], jnp.ones((2 * HD, local), NARROW)], axis=0
        )
        scores = mm(q_ref[...], keys)
        if masked:
            lane = lax.broadcasted_iota(jnp.int32, (LAT, local), 1) - (local - LAT)
            lat = lax.broadcasted_iota(jnp.int32, (LAT, local), 0)
            scores = jnp.where((lane <= lat) | jnp.logical_not(last), scores, -1e30)
        old = top_ref[:, 0:1]
        new = jnp.maximum(old, jnp.max(scores, axis=1, keepdims=True))
        probs = jnp.exp2(scores - new)
        p_high, p_low = halves(probs)
        dims = (((1,), (1,)), ((), ()))
        acc_ref[...] = acc_ref[...] * jnp.exp2(old - new) + (
            mm(p_high, vals, dims) + mm(p_low, vals, dims)
        )
        top_ref[...] = jnp.broadcast_to(new, top_ref.shape)

    def body(i, carry):
        step(i)
        return carry

    half = blocks // 2
    lax.fori_loop(0, half, body, 0)
    own.wait()
    for copy in wz_copies:
        copy.wait()
    for k, ss in enumerate(flat):
        line = wo_out_ref.at[:, s]
        copies.append(send(line, line, (wp_send, wp_recv), k, z * inner + ss, head))
    lax.fori_loop(half, blocks - 1, body, 0)
    step(blocks - 1, True)

    acc = acc_ref[...]
    state_ref[...] = jnp.concatenate(
        [acc[:, :HD] + acc[:, HD : 2 * HD], acc[:, 2 * HD : 2 * HD + 32], top_ref[:, 0:32]],
        axis=1,
    )
    rows = LAT // n_pos

    def latents_of(peer):
        return pl.ds(pl.multiple_of(peer * rows, rows), rows)

    for k, peer in enumerate(peers):
        copies.append(
            send(state_ref.at[latents_of(peer)], got_ref.at[me], (st_send, st_recv), k, peer, head)
        )
    got_ref[me] = state_ref[latents_of(me), :]
    for copy in copies:
        copy.wait()
    out_ref[...] = got_ref[...]


def mlp_kernel(
    n_pos, heads, outer, heads_dev, in_rows, states_ref, wo_ref, mlp_ref, out_ref,
    sums, lanes, full, other, other_got, red, red_got, mid, mid_got, last,
    s0, r0, s1, r1, s2, r2, s3, r3, s4, r4, s5, r5, s6, r6, s7, r7,
):
    inner = n_pos // outer
    me, head = lax.axis_index("pos"), lax.axis_index("head")
    z, s = me // inner, lax.rem(me, inner)
    cols = full.shape[-1]
    lat = n_pos * full.shape[3]
    siblings = [lax.rem(head + k, heads) for k in range(1, heads)]
    deep = [lax.rem(z + k, outer) for k in range(1, outer)]
    flat = [lax.rem(s + k, inner) for k in range(1, inner)]
    greet(
        [(me, h) for h in siblings]
        + [(zz * inner + s, head) for zz in deep]
        + [(z * inner + ss, head) for ss in flat]
    )

    parts = n_pos // heads_dev
    attended = []
    for slot in range(heads_dev):
        own = [states_ref[slot * parts + p] for p in range(parts)]
        top = own[0][:, 96:97]
        for state in own[1:]:
            top = jnp.maximum(top, state[:, 96:97])
        mixed = sum(state * jnp.exp2(state[:, 96:97] - top) for state in own)
        attended.append(mixed[:, :HD] / mixed[:, HD : HD + 1])
    attended = jnp.concatenate(attended, axis=1)
    sums[head] = mm3(attended, wo_ref[...], (((1,), (1,)), ((), ())))
    copies = [
        send(sums.at[head], sums.at[head], (s0, r0), k, me, h) for k, h in enumerate(siblings)
    ]
    for copy in copies:
        copy.wait()
    projected = sums[0]
    for h in range(1, heads):
        projected = projected + sums[h]
    normed = layer_norm(projected)
    for h in range(heads):
        lanes[h] = normed[:, h * cols : (h + 1) * cols]
    full[head, z, s] = lanes[head]

    mine = full.at[head, z, s]
    copies = [
        send(mine, mine, (s1, r1), k, zz * inner + s, head) for k, zz in enumerate(deep)
    ]
    for copy in copies:
        copy.wait()
    mine = full.at[head, :, s]
    copies = [
        send(mine, mine, (s2, r2), k, z * inner + ss, head) for k, ss in enumerate(flat)
    ]
    across = [
        send(mine, mine, (s3, r3), k * inner, me, h) for k, h in enumerate(siblings)
    ]
    for j, copy in enumerate(copies):
        copy.wait()
        came = full.at[head, :, lax.rem(s - (j + 1) + inner, inner)]
        across += [
            send(came, came, (s3, r3), k * inner + j + 1, me, h)
            for k, h in enumerate(siblings)
        ]

    def weights(h, first):
        mine = mlp_ref[pl.ds(h * (n_pos // heads), n_pos // heads), first : first + in_rows, :]
        return mine.reshape(cols, mine.shape[-1])

    def hidden_from(h):
        return mm3(full[h].reshape(lat, cols), weights(h, 0))

    hidden = hidden_from(head)
    for copy in across:
        copy.wait()
    for h in siblings:
        hidden = hidden + hidden_from(h)
    cube = hidden * hidden * hidden
    hidden = 0.5 * hidden * (1.0 + jnp.tanh(0.7978845608028654 * (hidden + 0.044715 * cube)))

    def down_to(h):
        return mm3(hidden, weights(h, in_rows), (((1,), (1,)), ((), ())))

    copies = []
    for k, h in enumerate(siblings):
        other[k] = down_to(h)
        copies.append(send(other.at[k], other_got.at[k], (s4, r4), k, me, h))
    total = down_to(head)
    for k, copy in enumerate(copies):
        copy.wait()
        total = total + other_got[k]
    red[...] = total.reshape(red.shape)

    copies = [
        send(red.at[:, ss], red_got.at[k], (s5, r5), k, z * inner + ss, head)
        for k, ss in enumerate(flat)
    ]
    total = red[:, s]
    for k, copy in enumerate(copies):
        copy.wait()
        total = total + red_got[k]
    mid[...] = total
    copies = [
        send(mid.at[zz], mid_got.at[k], (s6, r6), k, zz * inner + s, head)
        for k, zz in enumerate(deep)
    ]
    total = mid[z]
    for k, copy in enumerate(copies):
        copy.wait()
        total = total + mid_got[k]
    last[head] = total
    copies = [
        send(last.at[head], last.at[head], (s7, r7), k, me, h) for k, h in enumerate(siblings)
    ]
    for copy in copies:
        copy.wait()
    out_ref[...] = projected + jnp.concatenate([last[h] for h in range(heads)], axis=1)


def layer_norm(values):
    center = values - jnp.mean(values, axis=-1, keepdims=True)
    spread = jnp.mean(center * center, axis=-1, keepdims=True)
    return center * lax.rsqrt(spread + 1e-05)


def per_device(
    token_ids,
    token_table,
    row_table,
    col_table,
    chan_table,
    w_query,
    w_key,
    w_value,
    w_out,
    w_in,
    w_down,
):
    local = token_ids.shape[0]
    n_pos = lax.axis_size("pos")
    heads_dev = w_key.shape[1] // HD
    parts = n_pos // heads_dev
    depth = token_table.shape[1]
    outer = 4 if n_pos % 4 == 0 else 1
    inner = n_pos // outer
    vmem = pl.BlockSpec(memory_space=pltpu.VMEM)
    hbm = pl.BlockSpec(memory_space=pl.ANY)
    dma = pltpu.SemaphoreType.DMA

    def room(*shape):
        return pltpu.VMEM(shape, jnp.float32)

    ff_rows = w_in.shape[1] // n_pos
    lat_rows = LAT // n_pos
    moves = ff_rows % 128 == 0
    mlp_weights = jnp.concatenate([w_in, w_down.T])
    if not moves:
        mlp_kept = lax.all_to_all(
            mlp_weights.reshape(-1, n_pos, ff_rows).transpose(1, 0, 2),
            "pos", split_axis=0, concat_axis=0, tiled=True,
        )
        mlp_weights = jnp.zeros((8, 128), jnp.float32)
    mlp_shape = (n_pos, mlp_weights.shape[0], ff_rows) if moves else (8, 128)
    state_shape = (n_pos, lat_rows, 2 * HD)
    out_t = w_out.T
    spots = 2 * IMG + EXTRA
    states, whole_out, mlp_moved = pl.pallas_call(
        functools.partial(front_kernel, n_pos, parts, outer, moves),
        out_shape=[
            jax.ShapeDtypeStruct(state_shape, jnp.float32),
            jax.ShapeDtypeStruct((outer, inner) + out_t.shape, jnp.float32),
            jax.ShapeDtypeStruct(mlp_shape, jnp.float32),
        ],
        in_specs=[vmem] * 5 + [hbm] * 5,
        out_specs=[vmem, hbm, hbm],
        scratch_shapes=[
            room(spots, depth),
            pltpu.VMEM((spots, depth), NARROW),
            pltpu.VMEM((spots, depth), NARROW),
            room(3, depth, 2 * HD),
            room(n_pos, 2, local),
            room(LAT, 4 * HD),
            room(LAT, 128),
            pltpu.VMEM((4 * HD, spots), NARROW),
            pltpu.VMEM((LAT, 4 * HD), NARROW),
            room(LAT, 2 * HD),
            room(*state_shape),
            dma((3,)),
            dma((2,)),
        ]
        + [
            dma((count,))
            for count in (n_pos, outer, inner, n_pos, n_pos)
            for _ in range(2)
        ],
        compiler_params=pltpu.CompilerParams(
            vmem_limit_bytes=48 * 2**20, collective_id=1, has_side_effects=True
        ),
        cost_estimate=pl.CostEstimate(
            flops=20 * 10**9, bytes_accessed=8 * 2**20, transcendentals=4 * 2**20
        ),
    )(
        token_ids[None], token_table, row_table, col_table, chan_table,
        w_key, w_value, w_query, out_t, mlp_weights,
    )
    if moves:
        mlp_kept = mlp_moved
    whole_out = whole_out.reshape(depth, -1)

    heads = lax.axis_size("head")
    cols = depth // heads

    counts = [heads, outer, inner, heads * inner, heads, inner, outer, heads]
    return pl.pallas_call(
        functools.partial(mlp_kernel, n_pos, heads, outer, heads_dev, w_in.shape[0]),
        out_shape=jax.ShapeDtypeStruct((lat_rows, depth), jnp.float32),
        in_specs=[vmem] * 3,
        out_specs=vmem,
        scratch_shapes=[
            room(heads, lat_rows, depth),
            room(heads, lat_rows, cols),
            room(heads, outer, inner, lat_rows, cols),
            room(heads - 1, LAT, cols),
            room(heads - 1, LAT, cols),
            room(outer, inner, lat_rows, cols),
            room(inner - 1, outer, lat_rows, cols),
            room(outer, lat_rows, cols),
            room(outer - 1, lat_rows, cols),
            room(heads, lat_rows, cols),
        ]
        + [dma((count,)) for count in counts for _ in range(2)],
        compiler_params=pltpu.CompilerParams(
            vmem_limit_bytes=48 * 2**20, collective_id=2, has_side_effects=True
        ),
    )(states, whole_out, mlp_kept)


def solution(mesh):
    placed = (
        P("pos"),
        P(),
        P(),
        P(),
        P(),
        P(None, "head"),
        P(None, "head"),
        P(None, "head"),
        P("head", "pos"),
        P("pos", "head"),
        P("head", "pos"),
    )
    return jax.shard_map(
        per_device, mesh=mesh, in_specs=placed, out_specs=P("pos", None), check_vma=False
    )
```

```python
import functools

import jax
import jax.numpy as jnp
from jax import lax
from jax.experimental import pallas as pl
from jax.experimental.pallas import tpu as pltpu
from jax.sharding import PartitionSpec as P

HD = 64
IMG = 256
LAT = 512
LOG2E = 1.4426950408889634
ROWS_KEY = 24
ROWS_OWN = 16
ROWS_LAT = 16
CHAN_AT = ROWS_KEY + ROWS_OWN + ROWS_LAT
EXTRA = 128
NARROW = jnp.bfloat16


def halves(x):
    high = x.astype(NARROW)
    return high, (x - high.astype(jnp.float32)).astype(NARROW)


def mm(a, b, dims=(((1,), (0,)), ((), ()))):
    return lax.dot_general(a, b, dims, preferred_element_type=jnp.float32)


def mm3(a, b, dims=(((1,), (0,)), ((), ()))):
    a_high, a_low = halves(a)
    b_high, b_low = halves(b)
    return mm(a_high, b_high, dims) + (mm(a_high, b_low, dims) + mm(a_low, b_high, dims))


def send(src, dst, sems, at, pos, head):
    copy = pltpu.make_async_remote_copy(
        src_ref=src,
        dst_ref=dst,
        send_sem=sems[0].at[at],
        recv_sem=sems[1].at[at],
        device_id={"pos": pos, "head": head},
        device_id_type=pl.DeviceIdType.MESH,
    )
    copy.start()
    return copy


def greet(partners):
    barrier = pltpu.get_barrier_semaphore()
    for pos, head in partners:
        pl.semaphore_signal(
            barrier,
            inc=1,
            device_id={"pos": pos, "head": head},
            device_id_type=pl.DeviceIdType.MESH,
        )
    pl.semaphore_wait(barrier, len(partners))


def one_hot_t(ids, where, row_first, row_at):
    lanes = ids.shape[1]
    pixel = jnp.floor((where.astype(jnp.float32) + 0.5) * (1.0 / 3.0)).astype(jnp.int32)
    chan = where - 3 * pixel + CHAN_AT
    row = (pixel >> 8) - row_first + row_at
    column = pixel & (IMG - 1)
    tall = lax.broadcasted_iota(jnp.int32, (IMG, lanes), 0)
    short = lax.broadcasted_iota(jnp.int32, (EXTRA, lanes), 0)
    tok = jnp.where(tall == ids, 1.0, 0.0).astype(NARROW)
    col = jnp.where(tall == column, 1.0, 0.0).astype(NARROW)
    pair = jnp.where((short == row) | (short == chan), 1.0, 0.0).astype(NARROW)
    return jnp.concatenate([tok, col, pair], axis=0)


def layer_kernel(
    n_pos, heads, parts, outer, in_rows, moves,
    ids_ref, tok_ref, row_ref, col_ref, chan_ref, wk_ref, wv_ref, wq_ref, wo_ref, mlp_ref,
    out_ref, wo_out_ref, mlp_out_ref,
    sums, lanes, full, other, other_got, red, red_got, mid, mid_got, fin, tabs_ref, high_ref, low_ref, w_ref, ids_got, acc_ref, top_ref, kv_ref, q_ref, state_ref,
    got_ref, w_sem, own_sem, id_send, id_recv, wz_send, wz_recv, wp_send, wp_recv,
    mlp_send, mlp_recv, st_send, st_recv, s0, r0, s1, r1, s2, r2, s3, r3, s4, r4, s5, r5,
    s6, r6, s7, r7,
):
    inner = n_pos // outer
    me, head = lax.axis_index("pos"), lax.axis_index("head")
    z, s = me // inner, lax.rem(me, inner)
    peers = [lax.rem(me + k, n_pos) for k in range(1, n_pos)]
    deep = [lax.rem(z + k, outer) for k in range(1, outer)]
    flat = [lax.rem(s + k, inner) for k in range(1, inner)]
    siblings = [lax.rem(head + k, heads) for k in range(1, heads)]
    greet([(peer, head) for peer in peers] + [(me, h) for h in siblings])
    local = ids_ref.shape[1]
    total = local * n_pos
    span = total // parts
    slot, part = me // parts, lax.rem(me, parts)

    at = pl.multiple_of(slot // 2 * 2 * HD, 2 * HD)
    loads = []
    for k, ref in enumerate((wk_ref, wv_ref, wq_ref)):
        loads.append(
            pltpu.make_async_copy(ref.at[:, pl.ds(at, 2 * HD)], w_ref.at[k], w_sem.at[k])
        )
        loads[-1].start()

    def rows_from(start, count):
        first = start // (3 * IMG) // 8 * 8
        first = jnp.minimum(first, row_ref.shape[0] - count)
        return first, row_ref[pl.ds(pl.multiple_of(first, 8), count), :]

    key_first, key_rows = rows_from(part * span, ROWS_KEY)
    own_first, own_rows = rows_from(me * local, ROWS_OWN)
    lat_first, lat_rows = rows_from(jnp.int32(total - LAT), ROWS_LAT)
    tabs_ref[2 * IMG :, :] = jnp.zeros((EXTRA, tabs_ref.shape[1]), jnp.float32)
    tabs_ref[2 * IMG + CHAN_AT : 2 * IMG + CHAN_AT + 3, :] = chan_ref[...]
    extra = jnp.concatenate([key_rows, own_rows, lat_rows, tabs_ref[2 * IMG + CHAN_AT :, :]])
    for k, table in enumerate((tok_ref[...], col_ref[...], extra)):
        middle = table - jnp.mean(table, axis=1, keepdims=True)
        high, low = halves(middle)
        high_ref[k * IMG : k * IMG + table.shape[0], :] = high
        low_ref[k * IMG : k * IMG + table.shape[0], :] = low

    iota = lax.broadcasted_iota(jnp.int32, (1, local), 1)
    ids = ids_ref[...]
    pick = one_hot_t(ids, me * local + iota, own_first, ROWS_KEY)
    depth = tabs_ref.shape[1]
    square = jnp.zeros((1, local), jnp.float32)
    dims = (((0,), (0,)), ((), ()))
    for c in range(0, depth, 256):
        emb = mm(high_ref[:, c : c + 256], pick, dims) + mm(low_ref[:, c : c + 256], pick, dims)
        square = square + jnp.sum(emb * emb, axis=0, keepdims=True)
    inv = lax.rsqrt(square * (1.0 / depth) + 1e-05)
    ids_got[me] = jnp.concatenate([ids.astype(jnp.float32), inv], axis=0)
    id_copies = [
        send(ids_got.at[me], ids_got.at[me], (id_send, id_recv), k, peer, head)
        for k, peer in enumerate(peers)
    ]

    own = pltpu.make_async_copy(wo_ref, wo_out_ref.at[z, s], own_sem.at[0])
    own.start()
    wz_copies = [
        send(wo_ref, wo_out_ref.at[z, s], (wz_send, wz_recv), k, zz * inner + s, head)
        for k, zz in enumerate(deep)
    ]
    for load in loads:
        load.wait()
    even = lax.rem(slot, 2) == 0
    w = jnp.concatenate(
        [jnp.where(even, w_ref[k][:, :HD], w_ref[k][:, HD:]) for k in range(3)]
        + [jnp.zeros((depth, HD), jnp.float32)],
        axis=1,
    )
    w_high, w_low = halves(w)
    table = (
        mm(high_ref[...], w_high) + mm(high_ref[...], w_low) + mm(low_ref[...], w_high)
    )
    table_t = table.T
    kv_high, kv_low = halves(table_t[0 : 2 * HD])
    kv_ref[...] = jnp.concatenate([kv_high, kv_low], axis=0)
    q_high, q_low = halves(table_t[2 * HD : 3 * HD])
    top_ref[...] = jnp.full(top_ref.shape, -1e30, jnp.float32)
    acc_ref[...] = jnp.zeros(acc_ref.shape, jnp.float32)
    for copy in id_copies:
        copy.wait()

    late = ids_got[n_pos - 1][:, local - LAT :]
    lat_where = total - LAT + lax.broadcasted_iota(jnp.int32, (1, LAT), 1)
    lat_pick = one_hot_t(late[0:1].astype(jnp.int32), lat_where, lat_first, ROWS_KEY + ROWS_OWN)
    q_t = mm(q_high, lat_pick) + mm(q_low, lat_pick)
    q = (q_t * late[1:2] * (HD**-0.5 * LOG2E)).T
    q_high, q_low = halves(q)
    q_ref[...] = jnp.concatenate([q_high, q_high, q_low, q_low], axis=1)

    blocks = span // local
    last = part == parts - 1

    def step(i, masked=False):
        chunk = part * blocks + i
        got = ids_got[chunk]
        pick = one_hot_t(got[0:1].astype(jnp.int32), chunk * local + iota, key_first, 0)
        picked = mm(kv_ref[...], pick)
        both = (picked[0 : 2 * HD] + picked[2 * HD : 4 * HD]) * got[1:2]
        high, low = halves(both)
        keys = jnp.concatenate([high[:HD], low[:HD], high[:HD], low[:HD]], axis=0)
        vals = jnp.concatenate(
            [high[HD:], low[HD:], jnp.ones((2 * HD, local), NARROW)], axis=0
        )
        scores = mm(q_ref[...], keys)
        if masked:
            lane = lax.broadcasted_iota(jnp.int32, (LAT, local), 1) - (local - LAT)
            lat = lax.broadcasted_iota(jnp.int32, (LAT, local), 0)
            scores = jnp.where((lane <= lat) | jnp.logical_not(last), scores, -1e30)
        old = top_ref[:, 0:1]
        new = jnp.maximum(old, jnp.max(scores, axis=1, keepdims=True))
        probs = jnp.exp2(scores - new)
        p_high, p_low = halves(probs)
        dims = (((1,), (1,)), ((), ()))
        acc_ref[...] = acc_ref[...] * jnp.exp2(old - new) + (
            mm(p_high, vals, dims) + mm(p_low, vals, dims)
        )
        top_ref[...] = jnp.broadcast_to(new, top_ref.shape)

    def body(i, carry):
        step(i)
        return carry

    half = blocks // 4
    lax.fori_loop(0, half, body, 0)
    own.wait()
    for copy in wz_copies:
        copy.wait()
    line = wo_out_ref.at[:, s]
    wo_copies = [
        send(line, line, (wp_send, wp_recv), k, z * inner + ss, head)
        for k, ss in enumerate(flat)
    ]
    mlp_copies = []
    if moves:
        wide = mlp_ref.shape[1] // n_pos

        def slab(peer):
            return mlp_ref.at[:, pl.ds(pl.multiple_of(peer * wide, wide), wide)]

        for k, peer in enumerate(peers):
            mlp_copies.append(
                send(slab(peer), mlp_out_ref.at[me], (mlp_send, mlp_recv), k, peer, head)
            )
        kept = pltpu.make_async_copy(slab(me), mlp_out_ref.at[me], own_sem.at[1])
        kept.start()
        mlp_copies.append(kept)
    lax.fori_loop(half, blocks - 1, body, 0)
    step(blocks - 1, True)

    acc = acc_ref[...]
    state_ref[...] = jnp.concatenate(
        [acc[:, :HD] + acc[:, HD : 2 * HD], acc[:, 2 * HD : 2 * HD + 32], top_ref[:, 0:32]],
        axis=1,
    )
    rows = LAT // n_pos

    def latents_of(peer):
        return pl.ds(pl.multiple_of(peer * rows, rows), rows)

    copies = [
        send(state_ref.at[latents_of(peer)], got_ref.at[me], (st_send, st_recv), k, peer, head)
        for k, peer in enumerate(peers)
    ]
    got_ref[me] = state_ref[latents_of(me), :]
    for copy in copies + wo_copies:
        copy.wait()

    attended = []
    for first in range(0, n_pos, parts):
        own = [got_ref[first + p] for p in range(parts)]
        top = own[0][:, 96:97]
        for state in own[1:]:
            top = jnp.maximum(top, state[:, 96:97])
        mixed = sum(state * jnp.exp2(state[:, 96:97] - top) for state in own)
        attended.append(mixed[:, :HD] / mixed[:, HD : HD + 1])
    attended = jnp.concatenate(attended, axis=1)
    whole_out = wo_out_ref[...].reshape(depth, attended.shape[1])
    sums[head] = mm3(attended, whole_out, (((1,), (1,)), ((), ())))
    copies = [
        send(sums.at[head], sums.at[head], (s0, r0), k, me, h) for k, h in enumerate(siblings)
    ]
    for copy in copies:
        copy.wait()
    projected = sums[0]
    for h in range(1, heads):
        projected = projected + sums[h]
    normed = layer_norm(projected)
    cols = full.shape[-1]
    for h in range(heads):
        lanes[h] = normed[:, h * cols : (h + 1) * cols]
    full[head, z, s] = lanes[head]

    chunks = [lax.rem(z - k + outer, outer) for k in range(outer)]
    mine = full.at[head, z, s]
    arrive = [
        send(mine, mine, (s1, r1), k, zz * inner + s, head) for k, zz in enumerate(deep)
    ]
    in_plane, in_chip, halfway, spread = [], [], [], []

    def pass_on(k):
        if k > 0:
            arrive[k - 1].wait()
        came = full.at[head, chunks[k], s]
        in_plane.append(
            [
                send(came, came, (s2, r2), k * inner + j, z * inner + ss, head)
                for j, ss in enumerate(flat)
            ]
        )

    def to_chip(k):
        for copy in in_plane[k]:
            copy.wait()
        came = full.at[head, chunks[k]]
        in_chip.append(
            [
                send(came, came, (s3, r3), k * heads + j, me, h)
                for j, h in enumerate(siblings)
            ]
        )

    kept_ref = mlp_out_ref if moves else mlp_ref

    def weights(h, first):
        count = n_pos // heads
        held = kept_ref[pl.ds(h * count, count), first : first + in_rows, :]
        return held.reshape(cols, held.shape[-1])

    tall = LAT // outer

    def compute(k):
        for copy in in_chip[k]:
            copy.wait()
        hidden = None
        for h in [head] + siblings:
            term = mm3(full[h, chunks[k]].reshape(tall, cols), weights(h, 0))
            hidden = term if hidden is None else hidden + term
        cube = hidden * hidden * hidden
        hidden = 0.5 * hidden * (
            1.0 + jnp.tanh(0.7978845608028654 * (hidden + 0.044715 * cube))
        )
        dims = (((1,), (1,)), ((), ()))
        sent = []
        for j, h in enumerate(siblings):
            other[k, j] = mm3(hidden, weights(h, in_rows), dims)
            sent.append(
                send(other.at[k, j], other_got.at[k, j], (s4, r4), k * heads + j, me, h)
            )
        halfway.append(sent)
        red[k] = mm3(hidden, weights(head, in_rows), dims).reshape(red.shape[1:])

    def to_plane(k):
        whole = red[k].reshape(tall, cols)
        for j, copy in enumerate(halfway[k]):
            copy.wait()
            whole = whole + other_got[k, j]
        red[k] = whole.reshape(red.shape[1:])
        spread.append(
            [
                send(red.at[k, ss], red_got.at[k, j], (s5, r5), k * inner + j,
                     z * inner + ss, head)
                for j, ss in enumerate(flat)
            ]
        )

    final = []

    def to_owner(k):
        whole = red[k, s]
        for j, copy in enumerate(spread[k]):
            copy.wait()
            whole = whole + red_got[k, j]
        mid[k] = whole
        if k > 0:
            final.append(
                send(mid.at[k], mid_got.at[k], (s6, r6), k, chunks[k] * inner + s, head)
            )

    for k in range(outer):
        pass_on(k)
    to_chip(0)
    for copy in mlp_copies:
        copy.wait()
    for t in range(1, outer + 3):
        for stage, late_by in ((to_chip, 0), (compute, 1), (to_plane, 2), (to_owner, 3)):
            if 0 <= t - late_by < outer:
                stage(t - late_by)
    whole = mid[0]
    for k, copy in enumerate(final):
        copy.wait()
        whole = whole + mid_got[k + 1]
    fin[head] = whole
    copies = [
        send(fin.at[head], fin.at[head], (s7, r7), k, me, h) for k, h in enumerate(siblings)
    ]
    for copy in copies:
        copy.wait()
    out_ref[...] = projected + jnp.concatenate([fin[h] for h in range(heads)], axis=1)


def layer_norm(values):
    center = values - jnp.mean(values, axis=-1, keepdims=True)
    spread = jnp.mean(center * center, axis=-1, keepdims=True)
    return center * lax.rsqrt(spread + 1e-05)


def per_device(
    token_ids,
    token_table,
    row_table,
    col_table,
    chan_table,
    w_query,
    w_key,
    w_value,
    w_out,
    w_in,
    w_down,
):
    local = token_ids.shape[0]
    n_pos = lax.axis_size("pos")
    heads_dev = w_key.shape[1] // HD
    parts = n_pos // heads_dev
    depth = token_table.shape[1]
    outer = 4 if n_pos % 4 == 0 else 1
    inner = n_pos // outer
    vmem = pl.BlockSpec(memory_space=pltpu.VMEM)
    hbm = pl.BlockSpec(memory_space=pl.ANY)
    dma = pltpu.SemaphoreType.DMA

    def room(*shape):
        return pltpu.VMEM(shape, jnp.float32)

    ff_rows = w_in.shape[1] // n_pos
    lat_rows = LAT // n_pos
    moves = ff_rows % 128 == 0
    mlp_weights = jnp.concatenate([w_in, w_down.T])
    if not moves:
        mlp_kept = lax.all_to_all(
            mlp_weights.reshape(-1, n_pos, ff_rows).transpose(1, 0, 2),
            "pos", split_axis=0, concat_axis=0, tiled=True,
        )
        mlp_weights = mlp_kept
    mlp_shape = (n_pos, w_in.shape[0] * 2, ff_rows) if moves else (1, 8, 128)
    out_t = w_out.T
    spots = 2 * IMG + EXTRA
    heads = lax.axis_size("head")
    cols = depth // heads
    tall = LAT // outer
    counts = [n_pos, outer, inner, n_pos, n_pos]
    counts += [heads, outer, outer * inner, outer * heads, outer * heads, outer * inner]
    counts += [outer, heads]
    return pl.pallas_call(
        functools.partial(layer_kernel, n_pos, heads, parts, outer, w_in.shape[0], moves),
        out_shape=jax.ShapeDtypeStruct((lat_rows, depth), jnp.float32),
        in_specs=[vmem] * 5 + [hbm] * 4 + [hbm if moves else vmem],
        out_specs=vmem,
        scratch_shapes=[
            room(outer, inner, *out_t.shape),
            room(*mlp_shape),
            room(heads, lat_rows, depth),
            room(heads, lat_rows, cols),
            room(heads, outer, inner, lat_rows, cols),
            room(outer, heads - 1, tall, cols),
            room(outer, heads - 1, tall, cols),
            room(outer, inner, lat_rows, cols),
            room(outer, inner - 1, lat_rows, cols),
            room(outer, lat_rows, cols),
            room(outer, lat_rows, cols),
            room(heads, lat_rows, cols),
            room(spots, depth),
            pltpu.VMEM((spots, depth), NARROW),
            pltpu.VMEM((spots, depth), NARROW),
            room(3, depth, 2 * HD),
            room(n_pos, 2, local),
            room(LAT, 4 * HD),
            room(LAT, 128),
            pltpu.VMEM((4 * HD, spots), NARROW),
            pltpu.VMEM((LAT, 4 * HD), NARROW),
            room(LAT, 2 * HD),
            room(n_pos, lat_rows, 2 * HD),
            dma((3,)),
            dma((2,)),
        ]
        + [dma((count,)) for count in counts for _ in range(2)],
        compiler_params=pltpu.CompilerParams(
            vmem_limit_bytes=48 * 2**20, collective_id=1, has_side_effects=True
        ),
    )(
        token_ids[None], token_table, row_table, col_table, chan_table,
        w_key, w_value, w_query, out_t, mlp_weights,
    )


def solution(mesh):
    placed = (
        P("pos"),
        P(),
        P(),
        P(),
        P(),
        P(None, "head"),
        P(None, "head"),
        P(None, "head"),
        P("head", "pos"),
        P("pos", "head"),
        P("head", "pos"),
    )
    return jax.shard_map(
        per_device, mesh=mesh, in_specs=placed, out_specs=P("pos", None), check_vma=False
    )
```

```python
import functools

import jax
import jax.numpy as jnp
from jax import lax
from jax.experimental import pallas as pl
from jax.experimental.pallas import tpu as pltpu
from jax.sharding import PartitionSpec as P

HD = 64
IMG = 256
LAT = 512
LOG2E = 1.4426950408889634
ROWS_KEY = 24
ROWS_OWN = 16
ROWS_LAT = 16
CHAN_AT = ROWS_KEY + ROWS_OWN + ROWS_LAT
EXTRA = 128
NARROW = jnp.bfloat16


def halves(x):
    high = x.astype(NARROW)
    return high, (x - high.astype(jnp.float32)).astype(NARROW)


def mm(a, b, dims=(((1,), (0,)), ((), ()))):
    return lax.dot_general(a, b, dims, preferred_element_type=jnp.float32)


def mm3(a, b, dims=(((1,), (0,)), ((), ()))):
    a_high, a_low = halves(a)
    b_high, b_low = halves(b)
    return mm(a_high, b_high, dims) + (mm(a_high, b_low, dims) + mm(a_low, b_high, dims))


def send(src, dst, sems, at, pos, head):
    copy = pltpu.make_async_remote_copy(
        src_ref=src,
        dst_ref=dst,
        send_sem=sems[0].at[at],
        recv_sem=sems[1].at[at],
        device_id={"pos": pos, "head": head},
        device_id_type=pl.DeviceIdType.MESH,
    )
    copy.start()
    return copy


def greet(partners):
    barrier = pltpu.get_barrier_semaphore()
    for pos, head in partners:
        pl.semaphore_signal(
            barrier,
            inc=1,
            device_id={"pos": pos, "head": head},
            device_id_type=pl.DeviceIdType.MESH,
        )
    pl.semaphore_wait(barrier, len(partners))


def one_hot_t(ids, where, row_first, row_at):
    lanes = ids.shape[1]
    pixel = jnp.floor((where.astype(jnp.float32) + 0.5) * (1.0 / 3.0)).astype(jnp.int32)
    chan = where - 3 * pixel + CHAN_AT
    row = (pixel >> 8) - row_first + row_at
    column = pixel & (IMG - 1)
    tall = lax.broadcasted_iota(jnp.int32, (IMG, lanes), 0)
    short = lax.broadcasted_iota(jnp.int32, (EXTRA, lanes), 0)
    tok = jnp.where(tall == ids, 1.0, 0.0).astype(NARROW)
    col = jnp.where(tall == column, 1.0, 0.0).astype(NARROW)
    pair = jnp.where((short == row) | (short == chan), 1.0, 0.0).astype(NARROW)
    return jnp.concatenate([tok, col, pair], axis=0)


def layer_kernel(
    n_pos, heads, parts, outer, in_rows, moves,
    ids_ref, chan_ref, tok_hbm, row_hbm, col_hbm, wk_ref, wv_ref, wq_ref, wo_ref, in_ref,
    down_ref, out_ref, tok_ref, row_ref, col_ref, wo_out_ref, mlp_out_ref,
    sums, lanes, full, other, other_got, red, red_got, mid, mid_got, fin, tabs_ref, high_ref, low_ref, w_ref, ids_got, acc_ref, top_ref, kv_ref, q_ref, state_ref,
    got_ref, w_sem, own_sem, tab_sem, id_send, id_recv, wz_send, wz_recv, wp_send, wp_recv,
    mlp_send, mlp_recv, st_send, st_recv, s0, r0, s1, r1, s2, r2, s3, r3, s4, r4, s5, r5,
    s6, r6, s7, r7,
):
    inner = n_pos // outer
    me, head = lax.axis_index("pos"), lax.axis_index("head")
    z, s = me // inner, lax.rem(me, inner)
    peers = [lax.rem(me + k, n_pos) for k in range(1, n_pos)]
    deep = [lax.rem(z + k, outer) for k in range(1, outer)]
    flat = [lax.rem(s + k, inner) for k in range(1, inner)]
    siblings = [lax.rem(head + k, heads) for k in range(1, heads)]
    tables = []
    for k, (ref, room) in enumerate(((tok_hbm, tok_ref), (col_hbm, col_ref), (row_hbm, row_ref))):
        tables.append(pltpu.make_async_copy(ref, room, tab_sem.at[k]))
        tables[-1].start()
    greet([(peer, head) for peer in peers] + [(me, h) for h in siblings])
    own = pltpu.make_async_copy(wo_ref, wo_out_ref.at[z, s], own_sem.at[0])
    own.start()
    wz_copies = [
        send(wo_ref, wo_out_ref.at[z, s], (wz_send, wz_recv), k, zz * inner + s, head)
        for k, zz in enumerate(deep)
    ]
    local = ids_ref.shape[1]
    total = local * n_pos
    span = total // parts
    slot, part = me // parts, lax.rem(me, parts)

    at = pl.multiple_of(slot // 2 * 2 * HD, 2 * HD)
    loads = []
    for k, ref in enumerate((wk_ref, wv_ref, wq_ref)):
        loads.append(
            pltpu.make_async_copy(ref.at[:, pl.ds(at, 2 * HD)], w_ref.at[k], w_sem.at[k])
        )
        loads[-1].start()

    for load in tables:
        load.wait()

    def rows_from(start, count):
        first = start // (3 * IMG) // 8 * 8
        first = jnp.minimum(first, row_ref.shape[0] - count)
        return first, row_ref[pl.ds(pl.multiple_of(first, 8), count), :]

    key_first, key_rows = rows_from(part * span, ROWS_KEY)
    own_first, own_rows = rows_from(me * local, ROWS_OWN)
    lat_first, lat_rows = rows_from(jnp.int32(total - LAT), ROWS_LAT)
    tabs_ref[2 * IMG :, :] = jnp.zeros((EXTRA, tabs_ref.shape[1]), jnp.float32)
    tabs_ref[2 * IMG + CHAN_AT : 2 * IMG + CHAN_AT + 3, :] = chan_ref[...]
    extra = jnp.concatenate([key_rows, own_rows, lat_rows, tabs_ref[2 * IMG + CHAN_AT :, :]])
    for k, table in enumerate((tok_ref[...], col_ref[...], extra)):
        middle = table - jnp.mean(table, axis=1, keepdims=True)
        high, low = halves(middle)
        high_ref[k * IMG : k * IMG + table.shape[0], :] = high
        low_ref[k * IMG : k * IMG + table.shape[0], :] = low

    iota = lax.broadcasted_iota(jnp.int32, (1, local), 1)
    ids = ids_ref[...]
    pick = one_hot_t(ids, me * local + iota, own_first, ROWS_KEY)
    depth = tabs_ref.shape[1]
    square = jnp.zeros((1, local), jnp.float32)
    dims = (((0,), (0,)), ((), ()))
    for c in range(0, depth, 256):
        emb = mm(high_ref[:, c : c + 256], pick, dims) + mm(low_ref[:, c : c + 256], pick, dims)
        square = square + jnp.sum(emb * emb, axis=0, keepdims=True)
    inv = lax.rsqrt(square * (1.0 / depth) + 1e-05)
    ids_got[me] = jnp.concatenate([ids.astype(jnp.float32), inv], axis=0)
    id_copies = [
        send(ids_got.at[me], ids_got.at[me], (id_send, id_recv), k, peer, head)
        for k, peer in enumerate(peers)
    ]

    for load in loads:
        load.wait()
    even = lax.rem(slot, 2) == 0
    w = jnp.concatenate(
        [jnp.where(even, w_ref[k][:, :HD], w_ref[k][:, HD:]) for k in range(3)]
        + [jnp.zeros((depth, HD), jnp.float32)],
        axis=1,
    )
    w_high, w_low = halves(w)
    table = (
        mm(high_ref[...], w_high) + mm(high_ref[...], w_low) + mm(low_ref[...], w_high)
    )
    table_t = table.T
    kv_high, kv_low = halves(table_t[0 : 2 * HD])
    kv_ref[...] = jnp.concatenate([kv_high, kv_low], axis=0)
    q_high, q_low = halves(table_t[2 * HD : 3 * HD])
    top_ref[...] = jnp.full(top_ref.shape, -1e30, jnp.float32)
    acc_ref[...] = jnp.zeros(acc_ref.shape, jnp.float32)
    for copy in id_copies:
        copy.wait()

    late = ids_got[n_pos - 1][:, local - LAT :]
    lat_where = total - LAT + lax.broadcasted_iota(jnp.int32, (1, LAT), 1)
    lat_pick = one_hot_t(late[0:1].astype(jnp.int32), lat_where, lat_first, ROWS_KEY + ROWS_OWN)
    q_t = mm(q_high, lat_pick) + mm(q_low, lat_pick)
    q = (q_t * late[1:2] * (HD**-0.5 * LOG2E)).T
    q_high, q_low = halves(q)
    q_ref[...] = jnp.concatenate([q_high, q_high, q_low, q_low], axis=1)

    blocks = span // local
    last = part == parts - 1

    def step(i, masked=False):
        chunk = part * blocks + i
        got = ids_got[chunk]
        pick = one_hot_t(got[0:1].astype(jnp.int32), chunk * local + iota, key_first, 0)
        picked = mm(kv_ref[...], pick)
        both = (picked[0 : 2 * HD] + picked[2 * HD : 4 * HD]) * got[1:2]
        high, low = halves(both)
        keys = jnp.concatenate([high[:HD], low[:HD], high[:HD], low[:HD]], axis=0)
        vals = jnp.concatenate(
            [high[HD:], low[HD:], jnp.ones((2 * HD, local), NARROW)], axis=0
        )
        scores = mm(q_ref[...], keys)
        if masked:
            lane = lax.broadcasted_iota(jnp.int32, (LAT, local), 1) - (local - LAT)
            lat = lax.broadcasted_iota(jnp.int32, (LAT, local), 0)
            scores = jnp.where((lane <= lat) | jnp.logical_not(last), scores, -1e30)
        old = top_ref[:, 0:1]
        new = jnp.maximum(old, jnp.max(scores, axis=1, keepdims=True))
        probs = jnp.exp2(scores - new)
        p_high, p_low = halves(probs)
        dims = (((1,), (1,)), ((), ()))
        acc_ref[...] = acc_ref[...] * jnp.exp2(old - new) + (
            mm(p_high, vals, dims) + mm(p_low, vals, dims)
        )
        top_ref[...] = jnp.broadcast_to(new, top_ref.shape)

    def body(i, carry):
        step(i)
        return carry

    half = blocks // 8
    lax.fori_loop(0, half, body, 0)
    own.wait()
    for copy in wz_copies:
        copy.wait()
    line = wo_out_ref.at[:, s]
    wo_copies = [
        send(line, line, (wp_send, wp_recv), k, z * inner + ss, head)
        for k, ss in enumerate(flat)
    ]
    later = max(half, blocks * 3 // 8)
    lax.fori_loop(half, later, body, 0)
    mlp_copies = []
    if moves:
        wide = in_ref.shape[1] // n_pos
        for which, ref in enumerate((in_ref, down_ref)):

            def slab(peer, ref=ref):
                return ref.at[:, pl.ds(pl.multiple_of(peer * wide, wide), wide)]

            room = mlp_out_ref.at[me, which * in_rows : (which + 1) * in_rows]
            for k, peer in enumerate(peers):
                mlp_copies.append(
                    send(slab(peer), room, (mlp_send, mlp_recv), which * n_pos + k, peer, head)
                )
            kept = pltpu.make_async_copy(slab(me), room, own_sem.at[1 + which])
            kept.start()
            mlp_copies.append(kept)
    lax.fori_loop(later, blocks - 1, body, 0)
    step(blocks - 1, True)

    acc = acc_ref[...]
    state_ref[...] = jnp.concatenate(
        [acc[:, :HD] + acc[:, HD : 2 * HD], acc[:, 2 * HD : 2 * HD + 32], top_ref[:, 0:32]],
        axis=1,
    )
    rows = LAT // n_pos

    def latents_of(peer):
        return pl.ds(pl.multiple_of(peer * rows, rows), rows)

    copies = [
        send(state_ref.at[latents_of(peer)], got_ref.at[me], (st_send, st_recv), k, peer, head)
        for k, peer in enumerate(peers)
    ]
    got_ref[me] = state_ref[latents_of(me), :]
    for copy in copies + wo_copies:
        copy.wait()

    attended = []
    for first in range(0, n_pos, parts):
        own = [got_ref[first + p] for p in range(parts)]
        top = own[0][:, 96:97]
        for state in own[1:]:
            top = jnp.maximum(top, state[:, 96:97])
        mixed = sum(state * jnp.exp2(state[:, 96:97] - top) for state in own)
        attended.append(mixed[:, :HD] / mixed[:, HD : HD + 1])
    attended = jnp.concatenate(attended, axis=1)
    whole_out = wo_out_ref[...].reshape(depth, attended.shape[1])
    sums[head] = mm3(attended, whole_out, (((1,), (1,)), ((), ())))
    copies = [
        send(sums.at[head], sums.at[head], (s0, r0), k, me, h) for k, h in enumerate(siblings)
    ]
    for copy in copies:
        copy.wait()
    projected = sums[0]
    for h in range(1, heads):
        projected = projected + sums[h]
    normed = layer_norm(projected)
    cols = full.shape[-1]
    for h in range(heads):
        lanes[h] = normed[:, h * cols : (h + 1) * cols]
    full[head, z, s] = lanes[head]

    chunks = [lax.rem(z - k + outer, outer) for k in range(outer)]
    mine = full.at[head, z, s]
    arrive = [
        send(mine, mine, (s1, r1), k, zz * inner + s, head) for k, zz in enumerate(deep)
    ]
    in_plane, in_chip, halfway, spread = [], [], [], []

    def pass_on(k):
        if k > 0:
            arrive[k - 1].wait()
        came = full.at[head, chunks[k], s]
        in_plane.append(
            [
                send(came, came, (s2, r2), k * inner + j, z * inner + ss, head)
                for j, ss in enumerate(flat)
            ]
        )

    def to_chip(k):
        for copy in in_plane[k]:
            copy.wait()
        came = full.at[head, chunks[k]]
        in_chip.append(
            [
                send(came, came, (s3, r3), k * heads + j, me, h)
                for j, h in enumerate(siblings)
            ]
        )

    kept_ref = mlp_out_ref if moves else in_ref

    def weights(h, first):
        count = n_pos // heads
        held = kept_ref[pl.ds(h * count, count), first : first + in_rows, :]
        return held.reshape(cols, held.shape[-1])

    tall = LAT // outer

    def compute(k):
        for copy in in_chip[k]:
            copy.wait()
        hidden = None
        for h in [head] + siblings:
            term = mm3(full[h, chunks[k]].reshape(tall, cols), weights(h, 0))
            hidden = term if hidden is None else hidden + term
        cube = hidden * hidden * hidden
        hidden = 0.5 * hidden * (
            1.0 + jnp.tanh(0.7978845608028654 * (hidden + 0.044715 * cube))
        )
        dims = (((1,), (1,)), ((), ()))
        sent = []
        for j, h in enumerate(siblings):
            other[k, j] = mm3(hidden, weights(h, in_rows), dims)
            sent.append(
                send(other.at[k, j], other_got.at[k, j], (s4, r4), k * heads + j, me, h)
            )
        halfway.append(sent)
        red[k] = mm3(hidden, weights(head, in_rows), dims).reshape(red.shape[1:])

    def to_plane(k):
        whole = red[k].reshape(tall, cols)
        for j, copy in enumerate(halfway[k]):
            copy.wait()
            whole = whole + other_got[k, j]
        red[k] = whole.reshape(red.shape[1:])
        spread.append(
            [
                send(red.at[k, ss], red_got.at[k, j], (s5, r5), k * inner + j,
                     z * inner + ss, head)
                for j, ss in enumerate(flat)
            ]
        )

    final = []

    def to_owner(k):
        whole = red[k, s]
        for j, copy in enumerate(spread[k]):
            copy.wait()
            whole = whole + red_got[k, j]
        mid[k] = whole
        if k > 0:
            final.append(
                send(mid.at[k], mid_got.at[k], (s6, r6), k, chunks[k] * inner + s, head)
            )

    for k in range(outer):
        pass_on(k)
    to_chip(0)
    for copy in mlp_copies:
        copy.wait()
    for t in range(1, outer + 3):
        for stage, late_by in ((to_chip, 0), (compute, 1), (to_plane, 2), (to_owner, 3)):
            if 0 <= t - late_by < outer:
                stage(t - late_by)
    whole = mid[0]
    for k, copy in enumerate(final):
        copy.wait()
        whole = whole + mid_got[k + 1]
    fin[head] = whole
    copies = [
        send(fin.at[head], fin.at[head], (s7, r7), k, me, h) for k, h in enumerate(siblings)
    ]
    for copy in copies:
        copy.wait()
    out_ref[...] = projected + jnp.concatenate([fin[h] for h in range(heads)], axis=1)


def layer_norm(values):
    center = values - jnp.mean(values, axis=-1, keepdims=True)
    spread = jnp.mean(center * center, axis=-1, keepdims=True)
    return center * lax.rsqrt(spread + 1e-05)


def per_device(
    token_ids,
    token_table,
    row_table,
    col_table,
    chan_table,
    w_query,
    w_key,
    w_value,
    w_out,
    w_in,
    w_down,
):
    local = token_ids.shape[0]
    n_pos = lax.axis_size("pos")
    heads_dev = w_key.shape[1] // HD
    parts = n_pos // heads_dev
    depth = token_table.shape[1]
    outer = 4 if n_pos % 4 == 0 else 1
    inner = n_pos // outer
    vmem = pl.BlockSpec(memory_space=pltpu.VMEM)
    hbm = pl.BlockSpec(memory_space=pl.ANY)
    dma = pltpu.SemaphoreType.DMA

    def room(*shape):
        return pltpu.VMEM(shape, jnp.float32)

    ff_rows = w_in.shape[1] // n_pos
    lat_rows = LAT // n_pos
    moves = ff_rows % 128 == 0
    in_kept, down_t = w_in, w_down.T
    if not moves:
        in_kept = lax.all_to_all(
            jnp.concatenate([w_in, down_t]).reshape(-1, n_pos, ff_rows).transpose(1, 0, 2),
            "pos", split_axis=0, concat_axis=0, tiled=True,
        )
    mlp_shape = (n_pos, w_in.shape[0] * 2, ff_rows) if moves else (1, 8, 128)
    out_t = w_out.T
    spots = 2 * IMG + EXTRA
    heads = lax.axis_size("head")
    cols = depth // heads
    tall = LAT // outer
    counts = [n_pos, outer, inner, 2 * n_pos, n_pos]
    counts += [heads, outer, outer * inner, outer * heads, outer * heads, outer * inner]
    counts += [outer, heads]
    return pl.pallas_call(
        functools.partial(layer_kernel, n_pos, heads, parts, outer, w_in.shape[0], moves),
        out_shape=jax.ShapeDtypeStruct((lat_rows, depth), jnp.float32),
        in_specs=[vmem] * 2 + [hbm] * 7 + [hbm if moves else vmem, hbm],
        out_specs=vmem,
        scratch_shapes=[
            room(*token_table.shape),
            room(*row_table.shape),
            room(*col_table.shape),
            room(outer, inner, *out_t.shape),
            room(*mlp_shape),
            room(heads, lat_rows, depth),
            room(heads, lat_rows, cols),
            room(heads, outer, inner, lat_rows, cols),
            room(outer, heads - 1, tall, cols),
            room(outer, heads - 1, tall, cols),
            room(outer, inner, lat_rows, cols),
            room(outer, inner - 1, lat_rows, cols),
            room(outer, lat_rows, cols),
            room(outer, lat_rows, cols),
            room(heads, lat_rows, cols),
            room(spots, depth),
            pltpu.VMEM((spots, depth), NARROW),
            pltpu.VMEM((spots, depth), NARROW),
            room(3, depth, 2 * HD),
            room(n_pos, 2, local),
            room(LAT, 4 * HD),
            room(LAT, 128),
            pltpu.VMEM((4 * HD, spots), NARROW),
            pltpu.VMEM((LAT, 4 * HD), NARROW),
            room(LAT, 2 * HD),
            room(n_pos, lat_rows, 2 * HD),
            dma((3,)),
            dma((3,)),
            dma((3,)),
        ]
        + [dma((count,)) for count in counts for _ in range(2)],
        compiler_params=pltpu.CompilerParams(
            vmem_limit_bytes=56 * 2**20, collective_id=1, has_side_effects=True
        ),
    )(
        token_ids[None], chan_table, token_table, row_table, col_table,
        w_key, w_value, w_query, out_t, in_kept, down_t,
    )


def solution(mesh):
    placed = (
        P("pos"),
        P(),
        P(),
        P(),
        P(),
        P(None, "head"),
        P(None, "head"),
        P(None, "head"),
        P("head", "pos"),
        P("pos", "head"),
        P("head", "pos"),
    )
    return jax.shard_map(
        per_device, mesh=mesh, in_specs=placed, out_specs=P("pos", None), check_vma=False
    )
```

```python
import functools

import jax
import jax.numpy as jnp
from jax import lax
from jax.experimental import pallas as pl
from jax.experimental.pallas import tpu as pltpu
from jax.sharding import PartitionSpec as P

HD = 64
IMG = 256
LAT = 512
LOG2E = 1.4426950408889634
ROWS_KEY = 24
ROWS_OWN = 16
ROWS_LAT = 16
CHAN_AT = ROWS_KEY + ROWS_OWN + ROWS_LAT
EXTRA = 128
NARROW = jnp.bfloat16


def halves(x):
    high = x.astype(NARROW)
    return high, (x - high.astype(jnp.float32)).astype(NARROW)


def mm(a, b, dims=(((1,), (0,)), ((), ()))):
    return lax.dot_general(a, b, dims, preferred_element_type=jnp.float32)


def mm3(a, b, dims=(((1,), (0,)), ((), ()))):
    a_high, a_low = halves(a)
    b_high, b_low = halves(b)
    return mm(a_high, b_high, dims) + (mm(a_high, b_low, dims) + mm(a_low, b_high, dims))


def send(src, dst, sems, at, pos, head):
    copy = pltpu.make_async_remote_copy(
        src_ref=src,
        dst_ref=dst,
        send_sem=sems[0].at[at],
        recv_sem=sems[1].at[at],
        device_id={"pos": pos, "head": head},
        device_id_type=pl.DeviceIdType.MESH,
    )
    copy.start()
    return copy


def greet(partners):
    barrier = pltpu.get_barrier_semaphore()
    for pos, head in partners:
        pl.semaphore_signal(
            barrier,
            inc=1,
            device_id={"pos": pos, "head": head},
            device_id_type=pl.DeviceIdType.MESH,
        )
    pl.semaphore_wait(barrier, len(partners))


def one_hot_t(ids, where, row_first, row_at):
    lanes = ids.shape[1]
    pixel = jnp.floor((where.astype(jnp.float32) + 0.5) * (1.0 / 3.0)).astype(jnp.int32)
    chan = where - 3 * pixel + CHAN_AT
    row = (pixel >> 8) - row_first + row_at
    column = pixel & (IMG - 1)
    tall = lax.broadcasted_iota(jnp.int32, (IMG, lanes), 0)
    short = lax.broadcasted_iota(jnp.int32, (EXTRA, lanes), 0)
    tok = jnp.where(tall == ids, 1.0, 0.0).astype(NARROW)
    col = jnp.where(tall == column, 1.0, 0.0).astype(NARROW)
    pair = jnp.where((short == row) | (short == chan), 1.0, 0.0).astype(NARROW)
    return jnp.concatenate([tok, col, pair], axis=0)


def layer_kernel(
    n_pos, heads, parts, outer, in_rows, moves,
    ids_ref, chan_ref, tok_hbm, row_hbm, col_hbm, wk_ref, wv_ref, wq_ref, wo_ref, in_ref,
    down_ref, out_ref, tok_ref, row_ref, col_ref, wo_out_ref, mlp_out_ref,
    sums, lanes, full, other, other_got, red, red_got, mid, mid_got, fin, tabs_ref, high_ref, low_ref, w_ref, ids_got, acc_ref, top_ref, kv_ref, q_ref, state_ref,
    got_ref, w_sem, own_sem, tab_sem, id_send, id_recv, wz_send, wz_recv, wp_send, wp_recv,
    mlp_send, mlp_recv, st_send, st_recv, s0, r0, s1, r1, s2, r2, s3, r3, s4, r4, s5, r5,
    s6, r6, s7, r7,
):
    inner = n_pos // outer
    me, head = lax.axis_index("pos"), lax.axis_index("head")
    z, s = me // inner, lax.rem(me, inner)
    peers = [lax.rem(me + k, n_pos) for k in range(1, n_pos)]
    deep = [lax.rem(z + k, outer) for k in range(1, outer)]
    flat = [lax.rem(s + k, inner) for k in range(1, inner)]
    siblings = [lax.rem(head + k, heads) for k in range(1, heads)]
    tables = []
    for k, (ref, room) in enumerate(((tok_hbm, tok_ref), (col_hbm, col_ref), (row_hbm, row_ref))):
        tables.append(pltpu.make_async_copy(ref, room, tab_sem.at[k]))
        tables[-1].start()
    greet([(peer, head) for peer in peers] + [(me, h) for h in siblings])
    local = ids_ref.shape[1]
    total = local * n_pos
    span = total // parts
    slot, part = me // parts, lax.rem(me, parts)

    at = pl.multiple_of(slot // 2 * 2 * HD, 2 * HD)
    loads = []
    for k, ref in enumerate((wk_ref, wv_ref, wq_ref)):
        loads.append(
            pltpu.make_async_copy(ref.at[:, pl.ds(at, 2 * HD)], w_ref.at[k], w_sem.at[k])
        )
        loads[-1].start()

    for load in tables:
        load.wait()

    def rows_from(start, count):
        first = start // (3 * IMG) // 8 * 8
        first = jnp.minimum(first, row_ref.shape[0] - count)
        return first, row_ref[pl.ds(pl.multiple_of(first, 8), count), :]

    key_first, key_rows = rows_from(part * span, ROWS_KEY)
    own_first, own_rows = rows_from(me * local, ROWS_OWN)
    lat_first, lat_rows = rows_from(jnp.int32(total - LAT), ROWS_LAT)
    tabs_ref[2 * IMG :, :] = jnp.zeros((EXTRA, tabs_ref.shape[1]), jnp.float32)
    tabs_ref[2 * IMG + CHAN_AT : 2 * IMG + CHAN_AT + 3, :] = chan_ref[...]
    extra = jnp.concatenate([key_rows, own_rows, lat_rows, tabs_ref[2 * IMG + CHAN_AT :, :]])
    for k, table in enumerate((tok_ref[...], col_ref[...], extra)):
        middle = table - jnp.mean(table, axis=1, keepdims=True)
        high, low = halves(middle)
        high_ref[k * IMG : k * IMG + table.shape[0], :] = high
        low_ref[k * IMG : k * IMG + table.shape[0], :] = low

    iota = lax.broadcasted_iota(jnp.int32, (1, local), 1)
    ids = ids_ref[...]
    pick = one_hot_t(ids, me * local + iota, own_first, ROWS_KEY)
    depth = tabs_ref.shape[1]
    square = jnp.zeros((1, local), jnp.float32)
    dims = (((0,), (0,)), ((), ()))
    for c in range(0, depth, 256):
        emb = mm(high_ref[:, c : c + 256], pick, dims) + mm(low_ref[:, c : c + 256], pick, dims)
        square = square + jnp.sum(emb * emb, axis=0, keepdims=True)
    inv = lax.rsqrt(square * (1.0 / depth) + 1e-05)
    ids_got[me] = jnp.concatenate([ids.astype(jnp.float32), inv], axis=0)
    id_copies = [
        send(ids_got.at[me], ids_got.at[me], (id_send, id_recv), k, peer, head)
        for k, peer in enumerate(peers)
    ]

    own = pltpu.make_async_copy(wo_ref, wo_out_ref.at[z, s], own_sem.at[0])
    own.start()
    wz_copies = [
        send(wo_ref, wo_out_ref.at[z, s], (wz_send, wz_recv), k, zz * inner + s, head)
        for k, zz in enumerate(deep)
    ]

    for load in loads:
        load.wait()
    even = lax.rem(slot, 2) == 0
    w = jnp.concatenate(
        [jnp.where(even, w_ref[k][:, :HD], w_ref[k][:, HD:]) for k in range(3)]
        + [jnp.zeros((depth, HD), jnp.float32)],
        axis=1,
    )
    w_high, w_low = halves(w)
    table = (
        mm(high_ref[...], w_high) + mm(high_ref[...], w_low) + mm(low_ref[...], w_high)
    )
    table_t = table.T
    kv_high, kv_low = halves(table_t[0 : 2 * HD])
    kv_ref[...] = jnp.concatenate([kv_high, kv_low], axis=0)
    q_high, q_low = halves(table_t[2 * HD : 3 * HD])
    top_ref[...] = jnp.full(top_ref.shape, -1e30, jnp.float32)
    acc_ref[...] = jnp.zeros(acc_ref.shape, jnp.float32)
    for copy in id_copies:
        copy.wait()

    late = ids_got[n_pos - 1][:, local - LAT :]
    lat_where = total - LAT + lax.broadcasted_iota(jnp.int32, (1, LAT), 1)
    lat_pick = one_hot_t(late[0:1].astype(jnp.int32), lat_where, lat_first, ROWS_KEY + ROWS_OWN)
    q_t = mm(q_high, lat_pick) + mm(q_low, lat_pick)
    q = (q_t * late[1:2] * (HD**-0.5 * LOG2E)).T
    q_high, q_low = halves(q)
    q_ref[...] = jnp.concatenate([q_high, q_high, q_low, q_low], axis=1)

    blocks = span // local
    last = part == parts - 1

    def step(i, masked=False):
        chunk = part * blocks + i
        got = ids_got[chunk]
        pick = one_hot_t(got[0:1].astype(jnp.int32), chunk * local + iota, key_first, 0)
        picked = mm(kv_ref[...], pick)
        both = (picked[0 : 2 * HD] + picked[2 * HD : 4 * HD]) * got[1:2]
        high, low = halves(both)
        keys = jnp.concatenate([high[:HD], low[:HD], high[:HD], low[:HD]], axis=0)
        vals = jnp.concatenate(
            [high[HD:], low[HD:], jnp.ones((2 * HD, local), NARROW)], axis=0
        )
        scores = mm(q_ref[...], keys)
        if masked:
            lane = lax.broadcasted_iota(jnp.int32, (LAT, local), 1) - (local - LAT)
            lat = lax.broadcasted_iota(jnp.int32, (LAT, local), 0)
            scores = jnp.where((lane <= lat) | jnp.logical_not(last), scores, -1e30)
        old = top_ref[:, 0:1]
        new = jnp.maximum(old, jnp.max(scores, axis=1, keepdims=True))
        probs = jnp.exp2(scores - new)
        p_high, p_low = halves(probs)
        dims = (((1,), (1,)), ((), ()))
        acc_ref[...] = acc_ref[...] * jnp.exp2(old - new) + (
            mm(p_high, vals, dims) + mm(p_low, vals, dims)
        )
        top_ref[...] = jnp.broadcast_to(new, top_ref.shape)

    def body(i, carry):
        step(i)
        return carry

    half = blocks // 8
    lax.fori_loop(0, half, body, 0)
    own.wait()
    for copy in wz_copies:
        copy.wait()
    line = wo_out_ref.at[:, s]
    wo_copies = [
        send(line, line, (wp_send, wp_recv), k, z * inner + ss, head)
        for k, ss in enumerate(flat)
    ]
    later = half
    lax.fori_loop(half, later, body, 0)
    mlp_copies = []
    if moves:
        wide = in_ref.shape[1] // n_pos
        for which, ref in enumerate((in_ref, down_ref)):

            def slab(peer, ref=ref):
                return ref.at[:, pl.ds(pl.multiple_of(peer * wide, wide), wide)]

            room = mlp_out_ref.at[me, which * in_rows : (which + 1) * in_rows]
            for k, peer in enumerate(peers):
                mlp_copies.append(
                    send(slab(peer), room, (mlp_send, mlp_recv), which * n_pos + k, peer, head)
                )
            kept = pltpu.make_async_copy(slab(me), room, own_sem.at[1 + which])
            kept.start()
            mlp_copies.append(kept)
    lax.fori_loop(later, blocks - 1, body, 0)
    step(blocks - 1, True)

    acc = acc_ref[...]
    state_ref[...] = jnp.concatenate(
        [acc[:, :HD] + acc[:, HD : 2 * HD], acc[:, 2 * HD : 2 * HD + 32], top_ref[:, 0:32]],
        axis=1,
    )
    rows = LAT // n_pos

    def latents_of(peer):
        return pl.ds(pl.multiple_of(peer * rows, rows), rows)

    copies = [
        send(state_ref.at[latents_of(peer)], got_ref.at[me], (st_send, st_recv), k, peer, head)
        for k, peer in enumerate(peers)
    ]
    got_ref[me] = state_ref[latents_of(me), :]
    for copy in copies + wo_copies:
        copy.wait()

    attended = []
    for first in range(0, n_pos, parts):
        own = [got_ref[first + p] for p in range(parts)]
        top = own[0][:, 96:97]
        for state in own[1:]:
            top = jnp.maximum(top, state[:, 96:97])
        mixed = sum(state * jnp.exp2(state[:, 96:97] - top) for state in own)
        attended.append(mixed[:, :HD] / mixed[:, HD : HD + 1])
    attended = jnp.concatenate(attended, axis=1)
    whole_out = wo_out_ref[...].reshape(depth, attended.shape[1])
    sums[head] = mm3(attended, whole_out, (((1,), (1,)), ((), ())))
    copies = [
        send(sums.at[head], sums.at[head], (s0, r0), k, me, h) for k, h in enumerate(siblings)
    ]
    for copy in copies:
        copy.wait()
    projected = sums[0]
    for h in range(1, heads):
        projected = projected + sums[h]
    normed = layer_norm(projected)
    cols = full.shape[-1]
    for h in range(heads):
        lanes[h] = normed[:, h * cols : (h + 1) * cols]
    full[head, z, s] = lanes[head]

    chunks = [lax.rem(z - k + outer, outer) for k in range(outer)]
    mine = full.at[head, z, s]
    arrive = [
        send(mine, mine, (s1, r1), k, zz * inner + s, head) for k, zz in enumerate(deep)
    ]
    in_plane, in_chip, halfway, spread = [], [], [], []

    def pass_on(k):
        if k > 0:
            arrive[k - 1].wait()
        came = full.at[head, chunks[k], s]
        in_plane.append(
            [
                send(came, came, (s2, r2), k * inner + j, z * inner + ss, head)
                for j, ss in enumerate(flat)
            ]
        )

    def to_chip(k):
        for copy in in_plane[k]:
            copy.wait()
        came = full.at[head, chunks[k]]
        in_chip.append(
            [
                send(came, came, (s3, r3), k * heads + j, me, h)
                for j, h in enumerate(siblings)
            ]
        )

    kept_ref = mlp_out_ref if moves else in_ref

    def weights(h, first):
        count = n_pos // heads
        held = kept_ref[pl.ds(h * count, count), first : first + in_rows, :]
        return held.reshape(cols, held.shape[-1])

    tall = LAT // outer

    def compute(k):
        for copy in in_chip[k]:
            copy.wait()
        hidden = None
        for h in [head] + siblings:
            term = mm3(full[h, chunks[k]].reshape(tall, cols), weights(h, 0))
            hidden = term if hidden is None else hidden + term
        cube = hidden * hidden * hidden
        hidden = 0.5 * hidden * (
            1.0 + jnp.tanh(0.7978845608028654 * (hidden + 0.044715 * cube))
        )
        dims = (((1,), (1,)), ((), ()))
        sent = []
        for j, h in enumerate(siblings):
            other[k, j] = mm3(hidden, weights(h, in_rows), dims)
            sent.append(
                send(other.at[k, j], other_got.at[k, j], (s4, r4), k * heads + j, me, h)
            )
        halfway.append(sent)
        red[k] = mm3(hidden, weights(head, in_rows), dims).reshape(red.shape[1:])

    def to_plane(k):
        whole = red[k].reshape(tall, cols)
        for j, copy in enumerate(halfway[k]):
            copy.wait()
            whole = whole + other_got[k, j]
        red[k] = whole.reshape(red.shape[1:])
        spread.append(
            [
                send(red.at[k, ss], red_got.at[k, j], (s5, r5), k * inner + j,
                     z * inner + ss, head)
                for j, ss in enumerate(flat)
            ]
        )

    final = []

    def to_owner(k):
        whole = red[k, s]
        for j, copy in enumerate(spread[k]):
            copy.wait()
            whole = whole + red_got[k, j]
        mid[k] = whole
        if k > 0:
            final.append(
                send(mid.at[k], mid_got.at[k], (s6, r6), k, chunks[k] * inner + s, head)
            )

    for k in range(outer):
        pass_on(k)
    to_chip(0)
    for copy in mlp_copies:
        copy.wait()
    for t in range(1, outer + 3):
        for stage, late_by in ((to_chip, 0), (compute, 1), (to_plane, 2), (to_owner, 3)):
            if 0 <= t - late_by < outer:
                stage(t - late_by)
    whole = mid[0]
    for k, copy in enumerate(final):
        copy.wait()
        whole = whole + mid_got[k + 1]
    fin[head] = whole
    copies = [
        send(fin.at[head], fin.at[head], (s7, r7), k, me, h) for k, h in enumerate(siblings)
    ]
    for copy in copies:
        copy.wait()
    out_ref[...] = projected + jnp.concatenate([fin[h] for h in range(heads)], axis=1)


def layer_norm(values):
    center = values - jnp.mean(values, axis=-1, keepdims=True)
    spread = jnp.mean(center * center, axis=-1, keepdims=True)
    return center * lax.rsqrt(spread + 1e-05)


def per_device(
    token_ids,
    token_table,
    row_table,
    col_table,
    chan_table,
    w_query,
    w_key,
    w_value,
    w_out,
    w_in,
    w_down,
):
    local = token_ids.shape[0]
    n_pos = lax.axis_size("pos")
    heads_dev = w_key.shape[1] // HD
    parts = n_pos // heads_dev
    depth = token_table.shape[1]
    outer = 4 if n_pos % 4 == 0 else 1
    inner = n_pos // outer
    vmem = pl.BlockSpec(memory_space=pltpu.VMEM)
    hbm = pl.BlockSpec(memory_space=pl.ANY)
    dma = pltpu.SemaphoreType.DMA

    def room(*shape):
        return pltpu.VMEM(shape, jnp.float32)

    ff_rows = w_in.shape[1] // n_pos
    lat_rows = LAT // n_pos
    moves = ff_rows % 128 == 0
    in_kept, down_t = w_in, w_down.T
    if not moves:
        in_kept = lax.all_to_all(
            jnp.concatenate([w_in, down_t]).reshape(-1, n_pos, ff_rows).transpose(1, 0, 2),
            "pos", split_axis=0, concat_axis=0, tiled=True,
        )
    mlp_shape = (n_pos, w_in.shape[0] * 2, ff_rows) if moves else (1, 8, 128)
    out_t = w_out.T
    spots = 2 * IMG + EXTRA
    heads = lax.axis_size("head")
    cols = depth // heads
    tall = LAT // outer
    counts = [n_pos, outer, inner, 2 * n_pos, n_pos]
    counts += [heads, outer, outer * inner, outer * heads, outer * heads, outer * inner]
    counts += [outer, heads]
    return pl.pallas_call(
        functools.partial(layer_kernel, n_pos, heads, parts, outer, w_in.shape[0], moves),
        out_shape=jax.ShapeDtypeStruct((lat_rows, depth), jnp.float32),
        in_specs=[vmem] * 2 + [hbm] * 7 + [hbm if moves else vmem, hbm],
        out_specs=vmem,
        scratch_shapes=[
            room(*token_table.shape),
            room(*row_table.shape),
            room(*col_table.shape),
            room(outer, inner, *out_t.shape),
            room(*mlp_shape),
            room(heads, lat_rows, depth),
            room(heads, lat_rows, cols),
            room(heads, outer, inner, lat_rows, cols),
            room(outer, heads - 1, tall, cols),
            room(outer, heads - 1, tall, cols),
            room(outer, inner, lat_rows, cols),
            room(outer, inner - 1, lat_rows, cols),
            room(outer, lat_rows, cols),
            room(outer, lat_rows, cols),
            room(heads, lat_rows, cols),
            room(spots, depth),
            pltpu.VMEM((spots, depth), NARROW),
            pltpu.VMEM((spots, depth), NARROW),
            room(3, depth, 2 * HD),
            room(n_pos, 2, local),
            room(LAT, 4 * HD),
            room(LAT, 128),
            pltpu.VMEM((4 * HD, spots), NARROW),
            pltpu.VMEM((LAT, 4 * HD), NARROW),
            room(LAT, 2 * HD),
            room(n_pos, lat_rows, 2 * HD),
            dma((3,)),
            dma((3,)),
            dma((3,)),
        ]
        + [dma((count,)) for count in counts for _ in range(2)],
        compiler_params=pltpu.CompilerParams(
            vmem_limit_bytes=56 * 2**20, collective_id=1, has_side_effects=True
        ),
    )(
        token_ids[None], chan_table, token_table, row_table, col_table,
        w_key, w_value, w_query, out_t, in_kept, down_t,
    )


def solution(mesh):
    placed = (
        P("pos"),
        P(),
        P(),
        P(),
        P(),
        P(None, "head"),
        P(None, "head"),
        P(None, "head"),
        P("head", "pos"),
        P("pos", "head"),
        P("head", "pos"),
    )
    return jax.shard_map(
        per_device, mesh=mesh, in_specs=placed, out_specs=P("pos", None), check_vma=False
    )
```
